512 devices in a mesh: tm: 64 (over y, z), head: 4 (over x), farm: 2 (over core).
Axes of the slice: x: 4, y: 8, z: 8, core: 2. Of those that a mesh axis runs over, the one named last changes fastest.
Arguments:
- head_inputs: bfloat16 [2, 32768, 3072], P('farm', 'tm', 'head'), may hold values from -6 to 6
- b_proj: bfloat16 [2, 32768, 128], P('farm', 'tm'), may hold values from -0.625 to 0.625
- c_proj: bfloat16 [2, 32768, 128], P('farm', 'tm'), may hold values from -0.5 to 0.5
- log_decay: float32 [2, 32768, 48], P('farm', 'tm', 'head'), may hold values from -2 to 0
- skip_gain: float32 [48], P('head'), may hold values from 0.5 to 2
- w_out: bfloat16 [3072, 1536], P('head'), may hold values from -0.109375 to 0.109375
- norm_gain: float32 [1536], replicated, may hold values from 0.1 to 1.9
- owner_ids: int32 [2, 32768, 1], P('farm', ('tm', 'head')), may hold values from 0 to 127; in each aligned block of 128 rows (0 to 127, 128 to 255, ..., all dimensions but the last counted through in order) at most 2 rows name the same one
Outputs:
- regrouped: bfloat16 [128, 4, 128, 2, 1536], P(('tm', 'farm'), 'head')
The draws below stay inside these ranges and needn't reach their ends.
Inputs may be any that keep to these rules, and one draw needn't show every extreme that they name: `owner_ids`: in each aligned block of 128 rows no owner is named by more than 2 rows, and some block names an owner exactly 2 times.
All inputs are finite; a program needn't handle non-finite values.
Results may differ from the reference program's by a relative error of at most 0.02.
Values may be sent and summed in bfloat16 or wider, within the bound.
No kernel may reach another device: no remote copies, remote signals or barrier semaphores. Data moves between devices by JAX's collectives and lax.ppermute only.
A program may use at most 128 MiB of HBM per device.

```python
import math
import jax
import jax.numpy as jnp
import numpy as np
from jax import lax

D = 1536
HEADS = 48
HEAD_DIM = 64
STATE = 128
SPAN = 256
T_DEV = 512
INNER = 3072
WINDOW_STEPS = 32768
FARM_TOTAL = 2
ROWS_DEV = 128
OWNERS = 128
CAP = 2
N_TM = 64
N_HEAD = 4
N_FARM = 2


def draw_log_decay(key, part):
    random_subkeys = jax.random.split(key, 6)
    fast_share = 0.5
    shard_count = WINDOW_STEPS // T_DEV
    rate_low = min(3.0 / T_DEV, 0.1)
    rate_high = min(20.0 / T_DEV, 0.5)
    is_fast = jax.random.uniform(random_subkeys[0], (FARM_TOTAL, shard_count, 1, HEADS)) < fast_share
    fast_rate = jnp.exp(jax.random.uniform(random_subkeys[1], (FARM_TOTAL, shard_count, 1, HEADS), minval=jnp.log(rate_low), maxval=jnp.log(rate_high)))
    slow_rate = jax.random.uniform(random_subkeys[2], (FARM_TOTAL, 1, 1, HEADS), minval=0.2, maxval=0.6) / WINDOW_STEPS
    fading_speed = jnp.where(is_fast, fast_rate, slow_rate)
    fading_speed = jnp.broadcast_to(fading_speed, (FARM_TOTAL, shard_count, T_DEV, HEADS)).reshape(FARM_TOTAL, WINDOW_STEPS, HEADS)
    surface_texture = jnp.exp(jax.random.uniform(random_subkeys[3], (FARM_TOTAL, WINDOW_STEPS, HEADS), minval=-0.6931, maxval=0.6931))
    gust_position = jax.random.randint(random_subkeys[4], (FARM_TOTAL, 1, 3), 0, WINDOW_STEPS)
    gust_depths = jax.random.uniform(random_subkeys[5], (FARM_TOTAL, 1, 3), minval=0.22, maxval=0.5)
    step_locations = jnp.arange(WINDOW_STEPS)[None, :, None]
    gust_strength = jnp.sum(jnp.where(step_locations == gust_position, gust_depths, 0.0), axis=2, keepdims=True)
    return (-(fading_speed * surface_texture) - gust_strength).astype(jnp.float32)


def level_of(key, shape, shards, smallest, top_value):
    loudness = 1.0
    for axis_at, shards_of in shards:
        steps = jax.random.uniform(jax.random.fold_in(jax.random.fold_in(key, 6), axis_at), (shards_of,), jnp.float32, smallest / len(shards), top_value / len(shards))
        loudness = loudness * jnp.repeat(jnp.exp(steps), shape[axis_at] // shards_of).reshape((-1,) + (1,) * (len(shape) - 1 - axis_at))
    return loudness


def deal_out(key, own, number, rows, number_of, top, most, slope):
    sequence = jax.random.permutation(key, number_of)
    heavy_load, ordinary = load_shares(number_of, rows * top, most, slope, True), load_shares(number_of, rows * top, most, slope, False)
    places = jnp.arange(number_of)

    def named(lengths, offset_by):
        used = int((lengths > 0).sum())
        fixed = max(1, used // 4)
        passed = fixed + (places - fixed + offset_by * (used - fixed)) % max(1, number_of - fixed)
        return jnp.zeros((number_of,), jnp.int32).at[sequence[jnp.where(places < fixed, places, passed)]].set(jnp.asarray(lengths, jnp.int32))

    lengths = jnp.where(number % 4 == 0, named(heavy_load, number // 4), named(ordinary, number - number // 4 - 1))
    mixed = jax.random.permutation(jax.random.fold_in(own, 3), number_of)
    donor, sink = mixed[0:number_of // 2 * 2:2], mixed[1:number_of // 2 * 2:2]
    room = jnp.minimum(lengths[donor] - 1, most - lengths[sink]) // 2
    room = jnp.where((donor == sequence[0]) | (sink == sequence[0]) | (lengths[sink] == 0), 0, jnp.maximum(room, 0))
    passed = jax.random.randint(jax.random.fold_in(own, 4), (number_of // 2,), 0, 1 << 20) % (room + 1)
    lengths = lengths.at[donor].add(-passed).at[sink].add(passed)
    labels = jnp.searchsorted(jnp.cumsum(lengths), jnp.arange(rows * top), side="right").astype(jnp.int32)
    grid = labels.reshape(top, rows).T
    grid = grid[jax.random.permutation(jax.random.fold_in(own, 1), rows)]
    offset_by = jax.random.randint(jax.random.fold_in(own, 2), (rows, 1), 0, top)
    return jnp.take_along_axis(grid, (jnp.arange(top)[None, :] + offset_by) % top, axis=1)


def load_shares(number_of, total, reach, skew, full):
    loads = [(1 << 20) // math.isqrt(grade ** skew) + 1 for grade in range(1, number_of + 1)]
    largest = reach if full else min(reach, max(-(-total // number_of), total * loads[0] // sum(loads)))
    least = 1 if total - largest >= number_of - 1 else 0
    holding, spare = [largest] + [least] * (number_of - 1), total - largest - least * (number_of - 1)
    while spare > 0:
        candidates = [i for i in range(1, number_of) if holding[i] < largest] or [i for i in range(1, number_of) if holding[i] < reach]
        pool, remaining = sum([loads[i] for i in candidates]), spare
        for i in candidates:
            extra = min(reach - holding[i], max(1, remaining * loads[i] // pool), spare)
            holding[i] = holding[i] + extra
            spare = spare - extra
    return np.array(holding)


def normal_values(key, extent, scale, bound, cuts=(), kind=jnp.bfloat16):
    factor_of = level_of(key, extent, cuts, -0.22, 0.18) if cuts else 1.0
    drawn = jax.random.normal(key, extent, jnp.float32) * scale * factor_of
    return jnp.minimum(jnp.maximum(drawn, -bound), bound).astype(kind)


def setup_inputs(seed: int = 0) -> dict:
    splits = jax.random.split(jax.random.key(seed), 9)
    head_inputs = normal_values(splits[0], (FARM_TOTAL, WINDOW_STEPS, INNER), 1.0, 6.0, ((0, 2), (1, 64), (2, 4)))
    b_proj = normal_values(splits[1], (FARM_TOTAL, WINDOW_STEPS, STATE), (1.0 / WINDOW_STEPS ** 0.3), 0.625, ((0, 2), (1, 64)))
    c_proj = normal_values(splits[2], (FARM_TOTAL, WINDOW_STEPS, STATE), STATE ** -0.5, 0.5, ((0, 2), (1, 64)))
    log_decay = draw_log_decay(jax.random.fold_in(splits[8], 71), 0)
    skip_gain = jnp.clip(jnp.exp(math.log(2.0) - 1.3862944 * jax.random.uniform(splits[4], (HEADS,), jnp.float32) ** level_of(splits[4], (HEADS,), ((0, 4),), -0.2, 0.2)), 0.5, 2.0)
    w_out = normal_values(splits[5], (INNER, D), INNER ** -0.5, 0.109375, ((0, 4),))
    norm_gain = jnp.clip(1.0 + 0.18 * jax.random.normal(splits[6], (D,), jnp.float32), 0.1, 1.9)
    owner_ids_keys = jax.random.split(jax.random.fold_in(splits[7], 1), FARM_TOTAL * WINDOW_STEPS // ROWS_DEV)
    owner_ids_turns = jax.random.permutation(jax.random.fold_in(splits[7], 3), FARM_TOTAL * WINDOW_STEPS // ROWS_DEV)
    owner_ids = jax.vmap(lambda own, number: deal_out(jax.random.fold_in(splits[7], 2), own, number, ROWS_DEV, OWNERS, 1, CAP, 2))(owner_ids_keys, owner_ids_turns).reshape((FARM_TOTAL, WINDOW_STEPS, 1))
    return {"head_inputs": head_inputs, "b_proj": b_proj, "c_proj": c_proj, "log_decay": log_decay, "skip_gain": skip_gain, "w_out": w_out, "norm_gain": norm_gain, "owner_ids": owner_ids}


def span_step(carried, pieces):
    inputs_block, b_block, c_block, decay_block = pieces
    block_length = decay_block.shape[0]
    running_sum = jnp.cumsum(decay_block, axis=0)
    by_head = running_sum.T
    log_gaps = by_head[:, :, None] - by_head[:, None, :]
    causal = (jnp.arange(block_length)[:, None] >= jnp.arange(block_length)[None, :])[None]
    weights = jnp.where(causal, jnp.exp(jnp.where(causal, log_gaps, 0.0)), 0.0)
    scores = jnp.dot(c_block, b_block.T, precision=lax.Precision.HIGHEST)
    mixing = weights * scores[None]
    within = jnp.einsum('hts,shp->thp', mixing, inputs_block, precision=lax.Precision.HIGHEST)
    within = within + jnp.exp(running_sum)[:, :, None] * jnp.einsum('tn,hpn->thp', c_block, carried, precision=lax.Precision.HIGHEST)
    to_end = jnp.exp(running_sum[-1][None, :] - running_sum)
    updated = jnp.exp(running_sum[-1])[:, None, None] * carried + jnp.einsum('shp,sn->hpn', to_end[:, :, None] * inputs_block, b_block, precision=lax.Precision.HIGHEST)
    return (updated, within)

def one_farm(farm_args):
    inputs_farm, b_farm, c_farm, decay_farm = farm_args
    blocks = WINDOW_STEPS // SPAN
    pieces = (inputs_farm.astype(jnp.float32).reshape(blocks, SPAN, HEADS, HEAD_DIM), b_farm.astype(jnp.float32).reshape(blocks, SPAN, STATE), c_farm.astype(jnp.float32).reshape(blocks, SPAN, STATE), decay_farm.reshape(blocks, SPAN, HEADS))
    start_state = jnp.zeros((HEADS, HEAD_DIM, STATE), jnp.float32)
    final_state, outputs = lax.scan(span_step, start_state, pieces)
    return outputs.reshape(WINDOW_STEPS, HEADS, HEAD_DIM)

def reference(head_inputs, b_proj, c_proj, log_decay, skip_gain, w_out, norm_gain, owner_ids):
    ssd = lax.map(one_farm, (head_inputs, b_proj, c_proj, log_decay))
    ssd = ssd + skip_gain[None, None, :, None] * head_inputs.astype(jnp.float32).reshape(FARM_TOTAL, WINDOW_STEPS, HEADS, HEAD_DIM)
    mixed = ssd.reshape(FARM_TOTAL * WINDOW_STEPS, INNER).astype(jnp.bfloat16)
    projected = jnp.dot(mixed, w_out, preferred_element_type=jnp.float32)
    scale_rows = lax.rsqrt(lax.optimization_barrier(jnp.mean(projected * projected, axis=1, keepdims=True)) + 1e-06)
    normed = (projected * scale_rows * norm_gain[None, :]).astype(jnp.bfloat16)
    row_blocks = normed.reshape(FARM_TOTAL, N_TM, N_HEAD, ROWS_DEV, D)
    routes = owner_ids.reshape(FARM_TOTAL, N_TM, N_HEAD, ROWS_DEV)
    matches = (routes[..., None] == jnp.arange(OWNERS, dtype=jnp.int32)).astype(jnp.int32)
    earlier = jnp.cumsum(matches, axis=3) - matches
    slot_index = lax.optimization_barrier(jnp.sum(earlier * matches, axis=4))
    source = jnp.arange(N_TM, dtype=jnp.int32)[None, :, None, None] * N_FARM + jnp.arange(FARM_TOTAL, dtype=jnp.int32)[:, None, None, None]
    source = jnp.broadcast_to(source, routes.shape)
    piece_index = jnp.broadcast_to(jnp.arange(N_HEAD, dtype=jnp.int32)[None, None, :, None], routes.shape)
    regrouped = jnp.zeros((OWNERS, N_HEAD, OWNERS, CAP, D), jnp.bfloat16)
    regrouped = regrouped.at[routes, piece_index, source, slot_index].set(row_blocks)
    return regrouped
```

```python
import functools
import jax
import jax.numpy as jnp
from jax import lax
from jax.experimental import pallas as pl
from jax.experimental.pallas import tpu as pltpu
from jax.sharding import PartitionSpec as P

SPAN = 64
LANES = 128
F32 = jnp.float32
BF16 = jnp.bfloat16
FIRST = (((0,), (0,)), ((), ()))
LAST = (((1,), (1,)), ((), ()))


def mm(a, b):
    return jnp.dot(a, b, preferred_element_type=F32)


def split2(value):
    high = value.astype(BF16)
    return high, (value - high.astype(F32)).astype(BF16)


def split3(value):
    high = value.astype(BF16)
    rest = value - high.astype(F32)
    middle = rest.astype(BF16)
    return high, middle, (rest - middle.astype(F32)).astype(BF16)


def head_spread(rows, width, group):
    head = lax.broadcasted_iota(jnp.int32, (rows, width), 0) * group
    lane = lax.broadcasted_iota(jnp.int32, (rows, width), 1)
    return ((lane >= head) & (lane < head + group)).astype(BF16)


def spread(value, matrix):
    high, low = split2(value)
    return mm(high, matrix) + mm(low, matrix)


def state_kernel(x_ref, b_ref, decay_ref, out_ref, sums_ref, wx_ref, state_ref):
    steps, width = x_ref.shape
    heads = decay_ref.shape[1]
    spans = steps // SPAN
    parts = split3(decay_ref[...])
    row = lax.broadcasted_iota(jnp.int32, (SPAN, SPAN), 0)
    column = lax.broadcasted_iota(jnp.int32, (SPAN, SPAN), 1)
    lower = (row >= column).astype(BF16)
    matrix = head_spread(heads, width, width // heads)
    sums = []
    for k in range(spans):
        rows = slice(k * SPAN, (k + 1) * SPAN)
        local = sum(mm(lower, part[rows]) for part in parts)
        sums_ref[rows, :] = local
        sums.append(local)
    later = jnp.zeros((1, heads), F32)
    for k in reversed(range(spans)):
        rows = slice(k * SPAN, (k + 1) * SPAN)
        total = sums[k][SPAN - 1 : SPAN, :]
        weight = jnp.exp(total - sums[k] + later)
        wx_ref[rows, :] = (x_ref[rows, :].astype(F32) * spread(weight, matrix)).astype(BF16)
        later = later + total
    state_ref[...] = lax.dot_general(b_ref[...], wx_ref[...], FIRST, preferred_element_type=F32)
    parcels = out_ref.shape[0]
    depth = out_ref.shape[1]
    unit = head_spread(heads, LANES, 1)
    high, low = split2(later)
    tail = jnp.concatenate([mm(high, unit), mm(low, unit)], axis=0).astype(BF16)
    for k in range(parcels):
        out_ref[k, :, :width] = state_ref[k * depth : (k + 1) * depth, :].astype(BF16)
        out_ref[k, :, width:] = tail


def prefix_kernel(heads, in_ref, out_ref, log_ref):
    parcels, depth, width = out_ref.shape
    matrix = head_spread(LANES, width, width // heads)
    logs = in_ref[:, :, width:].reshape(parcels * depth, LANES)
    log_ref[...] = mm(logs, matrix)
    carried = jnp.zeros((depth, width), F32)
    for k in range(parcels):
        out_ref[k] = carried.astype(BF16)
        both = log_ref[k * depth : (k + 1) * depth, :]
        factor = jnp.exp(both[0:1, :] + both[1:2, :])
        carried = factor * carried + in_ref[k, :, :width].astype(F32)


def project_kernel(
    index_ref, x_ref, b_ref, c_ref, sums_ref, skip_ref, prior_ref, w_ref, *rest
):
    outs, (state_ref, mixed_ref) = rest[:-2], rest[-2:]
    steps, width = x_ref.shape
    heads = sums_ref.shape[1]
    spans = steps // SPAN
    pieces = len(outs)
    piece_spans = spans // pieces
    parcels, depth, _ = prior_ref.shape
    for k in range(parcels):
        state_ref[k * depth : (k + 1) * depth, :] = prior_ref[k].astype(F32)
    matrix = head_spread(heads, width, width // heads)
    row = lax.broadcasted_iota(jnp.int32, (SPAN, SPAN), 0)
    column = lax.broadcasted_iota(jnp.int32, (SPAN, SPAN), 1)
    causal = row >= column
    skip = spread(skip_ref[...], matrix)
    mine = index_ref[0]
    for k in range(spans):
        rows = slice(k * SPAN, (k + 1) * SPAN)
        local = sums_ref[rows, :]
        middle = 0.5 * local[SPAN - 1 : SPAN, :]
        up = spread(jnp.exp(local - middle), matrix)
        down = spread(jnp.exp(middle - local), matrix)
        half = up[SPAN - 1 : SPAN, :]
        x = x_ref[rows, :].astype(F32)
        b = b_ref[rows, :]
        c = c_ref[rows, :]
        scaled = (x * down).astype(BF16)
        scores = lax.dot_general(c, b, LAST, preferred_element_type=F32)
        scores = jnp.where(causal, scores, 0.0).astype(BF16)
        state = state_ref[...]
        y = mm(scores, scaled) + mm(c, (state * half).astype(BF16))
        y = up * y + skip * x
        slot = lax.rem(k // piece_spans - mine + pieces, pieces)
        start = pl.multiple_of((slot * piece_spans + k % piece_spans) * SPAN, SPAN)
        mixed_ref[pl.ds(start, SPAN), :] = y.astype(BF16)
        if k < spans - 1:
            update = lax.dot_general(b, scaled, FIRST, preferred_element_type=F32)
            state_ref[...] = half * (half * state + update)
    block = steps // pieces
    tile = 256
    for j in range(w_ref.shape[1] // tile):
        columns = slice(j * tile, (j + 1) * tile)
        product = mm(mixed_ref[...], w_ref[:, columns]).astype(BF16)
        for d in range(pieces):
            outs[d][:, columns] = product[d * block : (d + 1) * block, :]


def regroup_kernel(across_ref, down_ref, gain_ref, *rest):
    parts, out_ref = rest[:-1], rest[-1]
    owners, capacity, width = out_ref.shape
    rows = parts[0].shape[0]
    projected = sum(part[...].astype(F32) for part in parts)
    scale = lax.rsqrt(jnp.mean(projected * projected, axis=1, keepdims=True) + 1e-06)
    normed = (projected * scale * gain_ref[...]).astype(BF16)
    across = across_ref[...]
    earlier = lax.broadcasted_iota(jnp.int32, (rows, rows), 0) < lax.broadcasted_iota(
        jnp.int32, (rows, rows), 1
    )
    same = (down_ref[...] == across) & earlier
    slot = jnp.sum(same.astype(jnp.int32), axis=0, keepdims=True)
    target = across * capacity + slot
    place = lax.broadcasted_iota(jnp.int32, (owners * capacity, rows), 0)
    select = (place == target).astype(BF16)
    out_ref[...] = mm(select, normed).astype(BF16).reshape(owners, capacity, width)


def call(kernel, outs, scratch, flops, moved, *args, smem=0):
    vmem = pl.BlockSpec(memory_space=pltpu.VMEM)
    specs = [pl.BlockSpec(memory_space=pltpu.SMEM)] * smem + [vmem] * (len(args) - smem)
    return pl.pallas_call(
        kernel,
        out_shape=outs,
        in_specs=specs,
        out_specs=jax.tree.map(lambda _: vmem, outs),
        scratch_shapes=scratch,
        cost_estimate=pl.CostEstimate(flops=flops, bytes_accessed=moved, transcendentals=0),
        compiler_params=pltpu.CompilerParams(vmem_limit_bytes=32 * 1024 * 1024),
    )(*args)


def shards(head_inputs, b_proj, c_proj, log_decay, skip_gain, w_out, norm_gain, owner_ids):
    x, b, c, decays = head_inputs[0], b_proj[0], c_proj[0], log_decay[0]
    steps, width = x.shape
    heads = decays.shape[1]
    state_dim = b.shape[1]
    width_out = w_out.shape[1]
    times = lax.axis_size("tm")
    pieces = lax.axis_size("head")
    owners = times * lax.axis_size("farm")
    block = steps // pieces
    capacity = max(2, 2 * block // owners)
    depth = state_dim // times
    spec = jax.ShapeDtypeStruct
    parcel, sums = call(
        state_kernel,
        (spec((times, depth, width + LANES), BF16), spec((steps, heads), F32)),
        [pltpu.VMEM((steps, width), BF16), pltpu.VMEM((state_dim, width), F32)],
        2 * steps * width * state_dim,
        2 * steps * width,
        x,
        b,
        decays,
    )
    parcel = lax.all_to_all(parcel, "tm", split_axis=0, concat_axis=0, tiled=True)
    prior = call(
        functools.partial(prefix_kernel, heads),
        spec((times, depth, width), BF16),
        [pltpu.VMEM((times * depth, width), F32)],
        2 * state_dim * width * LANES,
        4 * state_dim * width,
        parcel,
    )
    prior = lax.all_to_all(prior, "tm", split_axis=0, concat_axis=0, tiled=True)
    index = lax.axis_index("head").astype(jnp.int32).reshape(1)
    parts = call(
        project_kernel,
        (spec((block, width_out), BF16),) * pieces,
        [pltpu.VMEM((state_dim, width), F32), pltpu.VMEM((steps, width), BF16)],
        2 * steps * width * (width_out + 2 * state_dim),
        2 * steps * (width + width_out) + 2 * width * width_out,
        index,
        x,
        b,
        c,
        sums,
        skip_gain[None, :],
        prior,
        w_out,
        smem=1,
    )
    ring = range(pieces)
    parts = [parts[0]] + [
        lax.ppermute(parts[d], "head", [(k, (k + d) % pieces) for k in ring])
        for d in range(1, pieces)
    ]
    outgoing = call(
        regroup_kernel,
        spec((owners, capacity, width_out), BF16),
        [],
        2 * owners * capacity * block * width_out,
        12 * block * width_out,
        owner_ids[0, :, 0][None, :],
        owner_ids[0],
        norm_gain[None, :],
        *parts,
    )
    result = lax.all_to_all(outgoing, ("tm", "farm"), split_axis=0, concat_axis=0, tiled=True)
    return result[None, None]


def solution(mesh):
    placed = (
        P("farm", "tm", "head"),
        P("farm", "tm", None),
        P("farm", "tm", None),
        P("farm", "tm", "head"),
        P("head"),
        P("head", None),
        P(),
        P("farm", ("tm", "head"), None),
    )
    return jax.shard_map(
        shards,
        mesh=mesh,
        in_specs=placed,
        out_specs=P(("tm", "farm"), "head", None, None, None),
        check_vma=False,
    )
```

```python
import functools
import jax
import jax.numpy as jnp
from jax import lax
from jax.experimental import pallas as pl
from jax.experimental.pallas import tpu as pltpu
from jax.sharding import PartitionSpec as P

SPAN = 64
LANES = 128
F32 = jnp.float32
BF16 = jnp.bfloat16
FIRST = (((0,), (0,)), ((), ()))
LAST = (((1,), (1,)), ((), ()))


def mm(a, b):
    return jnp.dot(a, b, preferred_element_type=F32)


def split2(value):
    high = value.astype(BF16)
    return high, (value - high.astype(F32)).astype(BF16)


def split3(value):
    high = value.astype(BF16)
    rest = value - high.astype(F32)
    middle = rest.astype(BF16)
    return high, middle, (rest - middle.astype(F32)).astype(BF16)


def head_spread(rows, width, group):
    head = lax.broadcasted_iota(jnp.int32, (rows, width), 0) * group
    lane = lax.broadcasted_iota(jnp.int32, (rows, width), 1)
    return ((lane >= head) & (lane < head + group)).astype(BF16)


def spread(value, matrix):
    high, low = split2(value)
    return lax.dot_general(high, matrix, FIRST, preferred_element_type=F32) + lax.dot_general(
        low, matrix, FIRST, preferred_element_type=F32
    )


def running(values, keep):
    length = values.shape[1]
    s = lax.broadcasted_iota(jnp.int32, (length, length), 0)
    t = lax.broadcasted_iota(jnp.int32, (length, length), 1)
    chosen = keep(s, t).astype(BF16)
    return sum(mm(part, chosen) for part in split3(values))


def fetch(pairs, sems):
    copies = [pltpu.make_async_copy(a, b, sems.at[i]) for i, (a, b) in enumerate(pairs)]
    for copy in copies:
        copy.start()
    return copies


def state_kernel(x_hbm, b_hbm, decay_ref, out_ref, x_ref, b_ref, wx_ref, state_ref, sems):
    copies = fetch(((x_hbm, x_ref), (b_hbm, b_ref)), sems)
    heads, _, steps = decay_ref.shape
    width = x_ref.shape[1]
    matrix = head_spread(heads, width, width // heads)
    later = jnp.zeros((heads, 1), F32)
    weights = [None] * (steps // LANES)
    for k in reversed(range(steps // LANES)):
        values = decay_ref[:, 0, k * LANES : (k + 1) * LANES]
        weights[k] = jnp.exp(running(values, lambda s, t: s > t) + later)
        later = later + jnp.sum(values, axis=1, keepdims=True)
    for copy in copies:
        copy.wait()
    for k, weight in enumerate(weights):
        rows = slice(k * LANES, (k + 1) * LANES)
        wx_ref[rows, :] = (x_ref[rows, :].astype(F32) * spread(weight, matrix)).astype(BF16)
    state_ref[...] = lax.dot_general(b_ref[...], wx_ref[...], FIRST, preferred_element_type=F32)
    parcels, depth, _ = out_ref.shape
    unit = head_spread(heads, LANES, 1)
    tail = [
        lax.dot_general(part, unit, FIRST, preferred_element_type=F32)[0:1]
        for part in split2(jnp.broadcast_to(later, (heads, LANES)))
    ]
    out_ref[:, :, :width] = state_ref[...].astype(BF16).reshape(parcels, depth, width)
    tail = jnp.concatenate(tail, axis=0).astype(BF16)
    for k in range(parcels):
        out_ref[k, :, width:] = tail


def prefix_kernel(heads, in_ref, out_ref, log_ref):
    parcels, depth, width = out_ref.shape
    matrix = head_spread(LANES, width, width // heads)
    logs = in_ref[:, :, width:].reshape(parcels * depth, LANES)
    log_ref[...] = mm(logs, matrix)
    carried = jnp.zeros((depth, width), F32)
    for k in range(parcels):
        out_ref[k] = carried.astype(BF16)
        both = log_ref[k * depth : (k + 1) * depth, :]
        factor = jnp.exp(both[0:1, :] + both[1:2, :])
        carried = factor * carried + in_ref[k, :, :width].astype(F32)


def local_kernel(
    x_ref, b_ref, c_ref, w_hbm, decay_ref, skip_ref, out_ref, w_ref, state_ref, sems
):
    copies = fetch(((w_hbm, w_ref),), sems)
    heads, _, steps = decay_ref.shape
    width = x_ref.shape[1]
    matrix = head_spread(heads, width, width // heads)
    row = lax.broadcasted_iota(jnp.int32, (SPAN, SPAN), 0)
    column = lax.broadcasted_iota(jnp.int32, (SPAN, SPAN), 1)
    causal = row >= column
    first = lax.broadcasted_iota(jnp.int32, (heads, LANES), 1) < SPAN
    skip = spread(jnp.broadcast_to(skip_ref[...], (heads, LANES)), matrix)[0:1]
    for k in range(steps // LANES):
        values = decay_ref[:, 0, k * LANES : (k + 1) * LANES]
        local = running(values, lambda s, t: (s <= t) & ((s < SPAN) == (t < SPAN)))
        middle = 0.5 * jnp.where(
            first, local[:, SPAN - 1 : SPAN], local[:, LANES - 1 : LANES]
        )
        ups = spread(jnp.exp(local - middle), matrix)
        downs = spread(jnp.exp(middle - local), matrix)
        for part in range(LANES // SPAN):
            inner = slice(part * SPAN, (part + 1) * SPAN)
            rows = slice(k * LANES + part * SPAN, k * LANES + (part + 1) * SPAN)
            up = ups[inner]
            half = up[SPAN - 1 : SPAN, :]
            x = x_ref[rows, :].astype(F32)
            b = b_ref[rows, :]
            c = c_ref[rows, :]
            scaled = (x * downs[inner]).astype(BF16)
            scores = lax.dot_general(c, b, LAST, preferred_element_type=F32)
            scores = jnp.where(causal, scores, 0.0).astype(BF16)
            y = mm(scores, scaled)
            update = lax.dot_general(b, scaled, FIRST, preferred_element_type=F32)
            if rows.start == 0:
                state_ref[...] = half * update
            else:
                state = state_ref[...]
                y = y + mm(c, (state * half).astype(BF16))
                state_ref[...] = half * (half * state + update)
            out_ref[rows, :width] = (up * y + skip * x).astype(BF16)
            out_ref[rows, width:] = c
    for copy in copies:
        copy.wait()


def project_kernel(local_ref, decay_ref, prior_ref, w_ref, out_hbm, mixed_ref, send_ref, sems):
    heads, _, steps = decay_ref.shape
    parcels, depth, width = prior_ref.shape
    pieces, block, width_out = send_ref.shape
    state = prior_ref[...].reshape(parcels * depth, width)
    matrix = head_spread(heads, width, width // heads)
    before = jnp.zeros((heads, 1), F32)
    reaches = []
    for k in range(steps // LANES):
        values = decay_ref[:, 0, k * LANES : (k + 1) * LANES]
        reaches.append(jnp.exp(running(values, lambda s, t: s <= t) + before))
        before = before + jnp.sum(values, axis=1, keepdims=True)
    for k, reach in enumerate(reaches):
        rows = slice(k * LANES, (k + 1) * LANES)
        carried = spread(reach, matrix) * mm(local_ref[rows, width:], state)
        mixed_ref[rows, :] = (local_ref[rows, :width].astype(F32) + carried).astype(BF16)
    tile = 256
    sends = []
    for j in range(width_out // tile):
        columns = slice(j * tile, (j + 1) * tile)
        product = mm(mixed_ref[...], w_ref[:, columns]).astype(BF16)
        for d in range(pieces):
            send_ref[d, :, columns] = product[d * block : (d + 1) * block, :]
        sends += fetch(
            ((send_ref.at[:, :, columns], out_hbm.at[:, :, columns]),), sems.at[pl.ds(j, 1)]
        )
    for send in sends:
        send.wait()


def regroup_kernel(across_ref, down_ref, gain_ref, parts_ref, out_ref):
    owners, capacity, width = out_ref.shape
    pieces, rows, _ = parts_ref.shape
    projected = sum(parts_ref[k].astype(F32) for k in range(pieces))
    scale = lax.rsqrt(jnp.mean(projected * projected, axis=1, keepdims=True) + 1e-06)
    normed = (projected * scale * gain_ref[...]).astype(BF16)
    across = across_ref[...]
    earlier = lax.broadcasted_iota(jnp.int32, (rows, rows), 0) < lax.broadcasted_iota(
        jnp.int32, (rows, rows), 1
    )
    same = (down_ref[...] == across) & earlier
    slot = jnp.sum(same.astype(jnp.int32), axis=0, keepdims=True)
    target = across * capacity + slot
    place = lax.broadcasted_iota(jnp.int32, (owners * capacity, rows), 0)
    select = (place == target).astype(BF16)
    out_ref[...] = mm(select, normed).astype(BF16).reshape(owners, capacity, width)


def call(kernel, outs, scratch, flops, moved, limit, *args, far=(), out_far=False):
    vmem = pl.BlockSpec(memory_space=pltpu.VMEM)
    hbm = pl.BlockSpec(memory_space=pltpu.HBM)
    return pl.pallas_call(
        kernel,
        out_shape=outs,
        in_specs=[hbm if k in far else vmem for k in range(len(args))],
        out_specs=jax.tree.map(lambda _: hbm if out_far else vmem, outs),
        scratch_shapes=scratch,
        cost_estimate=pl.CostEstimate(flops=flops, bytes_accessed=moved, transcendentals=0),
        compiler_params=pltpu.CompilerParams(vmem_limit_bytes=int(limit * 1024 * 1024)),
    )(*args)


def shards(head_inputs, b_proj, c_proj, log_decay, skip_gain, w_out, norm_gain, owner_ids):
    x, b, c, decays = head_inputs[0], b_proj[0], c_proj[0], log_decay.transpose(2, 0, 1)
    steps, width = x.shape
    heads = decays.shape[0]
    state_dim = b.shape[1]
    width_out = w_out.shape[1]
    times = lax.axis_size("tm")
    pieces = lax.axis_size("head")
    owners = times * lax.axis_size("farm")
    block = steps // pieces
    capacity = max(2, 2 * block // owners)
    depth = state_dim // times
    spec = jax.ShapeDtypeStruct
    wide = pltpu.VMEM((steps, width), BF16)
    narrow = pltpu.VMEM((steps, state_dim), BF16)
    state = pltpu.VMEM((state_dim, width), F32)
    parcel = call(
        state_kernel,
        spec((times, depth, width + LANES), BF16),
        [wide, narrow, wide, state, pltpu.SemaphoreType.DMA((2,))],
        2 * steps * width * state_dim,
        2 * steps * width,
        63.4,
        x,
        b,
        decays,
        far=(0, 1),
    )
    parcel = lax.all_to_all(parcel, "tm", split_axis=0, concat_axis=0, tiled=True)
    local, weights = call(
        local_kernel,
        (spec((steps, width + state_dim), BF16), spec(w_out.shape, BF16)),
        [state, pltpu.SemaphoreType.DMA((1,))],
        6 * steps * width * state_dim,
        8 * steps * width,
        24,
        x,
        b,
        c,
        w_out,
        decays,
        skip_gain[:, None],
        far=(3,),
    )
    prior = call(
        functools.partial(prefix_kernel, heads),
        spec((times, depth, width), BF16),
        [pltpu.VMEM((times * depth, width), F32)],
        2 * state_dim * width * LANES,
        4 * state_dim * width,
        16,
        parcel,
    )
    prior = lax.all_to_all(prior, "tm", split_axis=0, concat_axis=0, tiled=True)
    parts = call(
        project_kernel,
        spec((pieces, block, width_out), BF16),
        [
            wide,
            pltpu.VMEM((pieces, block, width_out), BF16),
            pltpu.SemaphoreType.DMA((width_out // 256,)),
        ],
        2 * steps * width * (width_out + state_dim),
        2 * steps * (width + width_out) + 2 * width * width_out,
        24,
        local,
        decays,
        prior,
        weights,
        out_far=True,
    )
    parts = lax.all_to_all(parts, "head", split_axis=0, concat_axis=0, tiled=True)
    outgoing = call(
        regroup_kernel,
        spec((owners, capacity, width_out), BF16),
        [],
        2 * owners * capacity * block * width_out,
        12 * block * width_out,
        16,
        owner_ids[0, :, 0][None, :],
        owner_ids[0],
        norm_gain[None, :],
        parts,
    )
    result = lax.all_to_all(outgoing, ("tm", "farm"), split_axis=0, concat_axis=0, tiled=True)
    return result[None, None]


def solution(mesh):
    placed = (
        P("farm", "tm", "head"),
        P("farm", "tm", None),
        P("farm", "tm", None),
        P("farm", "tm", "head"),
        P("head"),
        P("head", None),
        P(),
        P("farm", ("tm", "head"), None),
    )
    return jax.shard_map(
        shards,
        mesh=mesh,
        in_specs=placed,
        out_specs=P(("tm", "farm"), "head", None, None, None),
        check_vma=False,
    )
```

```python
import functools
import jax
import jax.numpy as jnp
from jax import lax
from jax.experimental import pallas as pl
from jax.experimental.pallas import tpu as pltpu
from jax.sharding import PartitionSpec as P

SPAN = 64
LANES = 128
ROWS = 16
F32 = jnp.float32
BF16 = jnp.bfloat16
FIRST = (((0,), (0,)), ((), ()))
LAST = (((1,), (1,)), ((), ()))


def mm(a, b):
    return jnp.dot(a, b, preferred_element_type=F32)


def split2(value):
    high = value.astype(BF16)
    return high, (value - high.astype(F32)).astype(BF16)


def split3(value):
    high = value.astype(BF16)
    rest = value - high.astype(F32)
    middle = rest.astype(BF16)
    return high, middle, (rest - middle.astype(F32)).astype(BF16)


def head_spread(rows, width, group):
    head = lax.broadcasted_iota(jnp.int32, (rows, width), 0) * group
    lane = lax.broadcasted_iota(jnp.int32, (rows, width), 1)
    return ((lane >= head) & (lane < head + group)).astype(BF16)


def spread(value, matrix):
    high, low = split2(value)
    return lax.dot_general(high, matrix, FIRST, preferred_element_type=F32) + lax.dot_general(
        low, matrix, FIRST, preferred_element_type=F32
    )


def running(values, keep):
    length = values.shape[1]
    s = lax.broadcasted_iota(jnp.int32, (length, length), 0)
    t = lax.broadcasted_iota(jnp.int32, (length, length), 1)
    chosen = keep(s, t).astype(BF16)
    return sum(mm(part, chosen) for part in split3(values))


def fetch(pairs, sems):
    copies = [pltpu.make_async_copy(a, b, sems.at[i]) for i, (a, b) in enumerate(pairs)]
    for copy in copies:
        copy.start()
    return copies


def state_kernel(
    x_hbm, b_hbm, decay_hbm, out_ref, x_ref, b_ref, decay_ref, wx_ref, state_ref, sems
):
    heads, _, steps = decay_ref.shape
    width = x_ref.shape[1]
    blocks = [slice(k * LANES, (k + 1) * LANES) for k in range(steps // LANES)]
    first, *others, last = fetch(
        [(decay_hbm, decay_ref)]
        + [(x_hbm.at[rows, :], x_ref.at[rows, :]) for rows in blocks]
        + [(b_hbm, b_ref)],
        sems,
    )
    matrix = head_spread(heads, width, width // heads)
    later = jnp.zeros((heads, 1), F32)
    weights = [None] * len(blocks)
    first.wait()
    for k in reversed(range(len(blocks))):
        values = decay_ref[:, 0, blocks[k]]
        weights[k] = jnp.exp(running(values, lambda s, t: s > t) + later)
        later = later + jnp.sum(values, axis=1, keepdims=True)
    for rows, weight, copy in zip(blocks, weights, others):
        weight = spread(weight, matrix)
        copy.wait()
        wx_ref[rows, :] = (x_ref[rows, :].astype(F32) * weight).astype(BF16)
    last.wait()
    state_ref[...] = lax.dot_general(b_ref[...], wx_ref[...], FIRST, preferred_element_type=F32)
    parcels, depth, _ = out_ref.shape
    unit = head_spread(heads, LANES, 1)
    tail = [
        lax.dot_general(part, unit, FIRST, preferred_element_type=F32)[0:1]
        for part in split2(jnp.broadcast_to(later, (heads, LANES)))
    ]
    out_ref[:, :, :width] = state_ref[...].astype(BF16).reshape(parcels, depth, width)
    tail = jnp.concatenate(tail, axis=0).astype(BF16)
    for k in range(parcels):
        out_ref[k, :, width:] = tail


def prefix_kernel(heads, in_ref, out_ref, log_ref):
    parcels, depth, width = out_ref.shape
    matrix = head_spread(LANES, width, width // heads)
    logs = in_ref[:, :, width:].reshape(parcels * depth, LANES)
    log_ref[...] = mm(logs, matrix)
    carried = jnp.zeros((depth, width), F32)
    for k in range(parcels):
        out_ref[k] = carried.astype(BF16)
        both = log_ref[k * depth : (k + 1) * depth, :]
        factor = jnp.exp(both[0:1, :] + both[1:2, :])
        carried = factor * carried + in_ref[k, :, :width].astype(F32)


def local_kernel(x_ref, b_ref, c_ref, decay_ref, skip_ref, out_ref, state_ref):
    heads, _, steps = decay_ref.shape
    width = x_ref.shape[1]
    matrix = head_spread(heads, width, width // heads)
    row = lax.broadcasted_iota(jnp.int32, (SPAN, SPAN), 0)
    column = lax.broadcasted_iota(jnp.int32, (SPAN, SPAN), 1)
    causal = row >= column
    first = lax.broadcasted_iota(jnp.int32, (heads, LANES), 1) < SPAN
    skip = spread(jnp.broadcast_to(skip_ref[...], (heads, LANES)), matrix)[0:1]
    before = jnp.zeros((heads, 1), F32)
    for k in range(steps // LANES):
        lanes = slice(k * LANES, (k + 1) * LANES)
        values = decay_ref[:, 0, lanes]
        reach = jnp.exp(running(values, lambda s, t: s <= t) + before)
        reach = jnp.concatenate([reach, jnp.zeros((ROWS - heads, LANES), F32)], axis=0)
        for part, half in enumerate(split2(reach)):
            out_ref[steps + part * ROWS : steps + (part + 1) * ROWS, lanes] = half
        before = before + jnp.sum(values, axis=1, keepdims=True)
        local = running(values, lambda s, t: (s <= t) & ((s < SPAN) == (t < SPAN)))
        middle = 0.5 * jnp.where(
            first, local[:, SPAN - 1 : SPAN], local[:, LANES - 1 : LANES]
        )
        ups = spread(jnp.exp(local - middle), matrix)
        downs = spread(jnp.exp(middle - local), matrix)
        for part in range(LANES // SPAN):
            inner = slice(part * SPAN, (part + 1) * SPAN)
            rows = slice(k * LANES + part * SPAN, k * LANES + (part + 1) * SPAN)
            up = ups[inner]
            half = up[SPAN - 1 : SPAN, :]
            x = x_ref[rows, :].astype(F32)
            b = b_ref[rows, :]
            c = c_ref[rows, :]
            scaled = (x * downs[inner]).astype(BF16)
            scores = lax.dot_general(c, b, LAST, preferred_element_type=F32)
            scores = jnp.where(causal, scores, 0.0).astype(BF16)
            y = mm(scores, scaled)
            update = lax.dot_general(b, scaled, FIRST, preferred_element_type=F32)
            if rows.start == 0:
                state_ref[...] = half * update
            else:
                state = state_ref[...]
                y = y + mm(c, (state * half).astype(BF16))
                state_ref[...] = half * (half * state + update)
            out_ref[rows, :width] = (up * y + skip * x).astype(BF16)
            out_ref[rows, width:] = c


def early_kernel(
    capacity, w_hbm, across_ref, down_ref, gain_ref, w_ref, target_ref, gain_out_ref, sems
):
    (copy,) = fetch(((w_hbm, w_ref),), sems)
    across = across_ref[...]
    rows = across.shape[1]
    earlier = lax.broadcasted_iota(jnp.int32, (rows, rows), 0) < lax.broadcasted_iota(
        jnp.int32, (rows, rows), 1
    )
    same = (down_ref[...] == across) & earlier
    slot = jnp.sum(same.astype(jnp.int32), axis=0, keepdims=True)
    target_ref[...] = across * capacity + slot
    gain_out_ref[...] = gain_ref[...]
    copy.wait()


def project_kernel(heads, local_ref, prior_ref, w_ref, out_ref, mixed_ref):
    steps = mixed_ref.shape[0]
    parcels, depth, width = prior_ref.shape
    pieces, block, width_out = out_ref.shape
    state = prior_ref[...].reshape(parcels * depth, width)
    matrix = head_spread(ROWS, width, width // heads)
    for k in range(steps // LANES):
        rows = slice(k * LANES, (k + 1) * LANES)
        reach = sum(
            lax.dot_general(
                local_ref[steps + part * ROWS : steps + (part + 1) * ROWS, rows],
                matrix,
                FIRST,
                preferred_element_type=F32,
            )
            for part in range(2)
        )
        carried = reach * mm(local_ref[rows, width:], state)
        mixed_ref[rows, :] = (local_ref[rows, :width].astype(F32) + carried).astype(BF16)
    tile = 256
    for j in range(width_out // tile):
        columns = slice(j * tile, (j + 1) * tile)
        product = mm(mixed_ref[...], w_ref[:, columns]).astype(BF16)
        for d in range(pieces):
            out_ref[d, :, columns] = product[d * block : (d + 1) * block, :]


def regroup_kernel(target_ref, gain_ref, parts_ref, out_ref):
    owners, capacity, width = out_ref.shape
    pieces, rows, _ = parts_ref.shape
    projected = sum(parts_ref[k].astype(F32) for k in range(pieces))
    scale = lax.rsqrt(jnp.mean(projected * projected, axis=1, keepdims=True) + 1e-06)
    normed = (projected * scale * gain_ref[...]).astype(BF16)
    place = lax.broadcasted_iota(jnp.int32, (owners * capacity, rows), 0)
    select = (place == target_ref[...]).astype(BF16)
    out_ref[...] = mm(select, normed).astype(BF16).reshape(owners, capacity, width)


def call(kernel, outs, scratch, flops, moved, limit, *args, far=()):
    vmem = pl.BlockSpec(memory_space=pltpu.VMEM)
    hbm = pl.BlockSpec(memory_space=pltpu.HBM)
    return pl.pallas_call(
        kernel,
        out_shape=outs,
        in_specs=[hbm if k in far else vmem for k in range(len(args))],
        out_specs=jax.tree.map(lambda _: vmem, outs),
        scratch_shapes=scratch,
        cost_estimate=pl.CostEstimate(flops=flops, bytes_accessed=moved, transcendentals=0),
        compiler_params=pltpu.CompilerParams(vmem_limit_bytes=int(limit * 1024 * 1024)),
    )(*args)


def shards(head_inputs, b_proj, c_proj, log_decay, skip_gain, w_out, norm_gain, owner_ids):
    x, b, c, decays = head_inputs[0], b_proj[0], c_proj[0], log_decay.transpose(2, 0, 1)
    steps, width = x.shape
    heads = decays.shape[0]
    state_dim = b.shape[1]
    width_out = w_out.shape[1]
    times = lax.axis_size("tm")
    pieces = lax.axis_size("head")
    owners = times * lax.axis_size("farm")
    block = steps // pieces
    capacity = max(2, 2 * block // owners)
    depth = state_dim // times
    spec = jax.ShapeDtypeStruct
    wide = pltpu.VMEM((steps, width), BF16)
    narrow = pltpu.VMEM((steps, state_dim), BF16)
    state = pltpu.VMEM((state_dim, width), F32)
    parcel = call(
        state_kernel,
        spec((times, depth, width + LANES), BF16),
        [
            wide,
            narrow,
            pltpu.VMEM(decays.shape, F32),
            wide,
            state,
            pltpu.SemaphoreType.DMA((2 + steps // LANES,)),
        ],
        2 * steps * width * state_dim,
        2 * steps * width,
        63.4,
        x,
        b,
        decays,
        far=(0, 1, 2),
    )
    parcel = lax.all_to_all(parcel, "tm", split_axis=0, concat_axis=0, tiled=True)
    local = call(
        local_kernel,
        spec((steps + 2 * ROWS, width + state_dim), BF16),
        [state],
        6 * steps * width * state_dim,
        8 * steps * width,
        24,
        x,
        b,
        c,
        decays,
        skip_gain[:, None],
    )
    parcel, local, w_late = lax.optimization_barrier((parcel, local, w_out))
    weights, target, gain = call(
        functools.partial(early_kernel, capacity),
        (spec(w_out.shape, BF16), spec((1, block), jnp.int32), spec((1, width_out), F32)),
        [pltpu.SemaphoreType.DMA((1,))],
        0,
        4 * width * width_out,
        16,
        w_late,
        owner_ids[0, :, 0][None, :],
        owner_ids[0],
        norm_gain[None, :],
        far=(0,),
    )
    prior = call(
        functools.partial(prefix_kernel, heads),
        spec((times, depth, width), BF16),
        [pltpu.VMEM((times * depth, width), F32)],
        2 * state_dim * width * LANES,
        4 * state_dim * width,
        16,
        parcel,
    )
    prior = lax.all_to_all(prior, "tm", split_axis=0, concat_axis=0, tiled=True)
    parts = call(
        functools.partial(project_kernel, heads),
        spec((pieces, block, width_out), BF16),
        [wide],
        2 * steps * width * (width_out + state_dim),
        2 * steps * (width + width_out) + 2 * width * width_out,
        24,
        local,
        prior,
        weights,
    )
    parts = lax.all_to_all(parts, "head", split_axis=0, concat_axis=0, tiled=True)
    outgoing = call(
        regroup_kernel,
        spec((owners, capacity, width_out), BF16),
        [],
        2 * owners * capacity * block * width_out,
        12 * block * width_out,
        16,
        target,
        gain,
        parts,
    )
    result = lax.all_to_all(outgoing, ("tm", "farm"), split_axis=0, concat_axis=0, tiled=True)
    return result[None, None]


def solution(mesh):
    placed = (
        P("farm", "tm", "head"),
        P("farm", "tm", None),
        P("farm", "tm", None),
        P("farm", "tm", "head"),
        P("head"),
        P("head", None),
        P(),
        P("farm", ("tm", "head"), None),
    )
    return jax.shard_map(
        shards,
        mesh=mesh,
        in_specs=placed,
        out_specs=P(("tm", "farm"), "head", None, None, None),
        check_vma=False,
    )
```

```python
import functools
import jax
import jax.numpy as jnp
from jax import lax
from jax.experimental import pallas as pl
from jax.experimental.pallas import tpu as pltpu
from jax.sharding import PartitionSpec as P

SPAN = 64
LANES = 128
ROWS = 16
F32 = jnp.float32
BF16 = jnp.bfloat16
FIRST = (((0,), (0,)), ((), ()))
LAST = (((1,), (1,)), ((), ()))


def mm(a, b):
    return jnp.dot(a, b, preferred_element_type=F32)


def split2(value):
    high = value.astype(BF16)
    return high, (value - high.astype(F32)).astype(BF16)


def split3(value):
    high = value.astype(BF16)
    rest = value - high.astype(F32)
    middle = rest.astype(BF16)
    return high, middle, (rest - middle.astype(F32)).astype(BF16)


def head_spread(rows, width, group):
    head = lax.broadcasted_iota(jnp.int32, (rows, width), 0) * group
    lane = lax.broadcasted_iota(jnp.int32, (rows, width), 1)
    return ((lane >= head) & (lane < head + group)).astype(BF16)


def spread(value, matrix):
    high, low = split2(value)
    return lax.dot_general(high, matrix, FIRST, preferred_element_type=F32) + lax.dot_general(
        low, matrix, FIRST, preferred_element_type=F32
    )


def running(values, keep):
    length = values.shape[1]
    s = lax.broadcasted_iota(jnp.int32, (length, length), 0)
    t = lax.broadcasted_iota(jnp.int32, (length, length), 1)
    chosen = keep(s, t).astype(BF16)
    return sum(mm(part, chosen) for part in split3(values))


def fetch(pairs, sems):
    copies = [pltpu.make_async_copy(a, b, sems.at[i]) for i, (a, b) in enumerate(pairs)]
    for copy in copies:
        copy.start()
    return copies


def state_kernel(
    x_hbm, b_hbm, decay_hbm, out_ref, x_ref, b_ref, decay_ref, wx_ref, state_ref, sems
):
    heads, _, steps = decay_ref.shape
    width = x_ref.shape[1]
    blocks = [slice(k * LANES, (k + 1) * LANES) for k in range(steps // LANES)]
    first, *others, last = fetch(
        [(decay_hbm, decay_ref)]
        + [(x_hbm.at[rows, :], x_ref.at[rows, :]) for rows in blocks]
        + [(b_hbm, b_ref)],
        sems,
    )
    matrix = head_spread(heads, width, width // heads)
    later = jnp.zeros((heads, 1), F32)
    weights = [None] * len(blocks)
    first.wait()
    for k in reversed(range(len(blocks))):
        values = decay_ref[:, 0, blocks[k]]
        weights[k] = jnp.exp(running(values, lambda s, t: s > t) + later)
        later = later + jnp.sum(values, axis=1, keepdims=True)
    for rows, weight, copy in zip(blocks, weights, others):
        weight = spread(weight, matrix)
        copy.wait()
        wx_ref[rows, :] = (x_ref[rows, :].astype(F32) * weight).astype(BF16)
    last.wait()
    state_ref[...] = lax.dot_general(b_ref[...], wx_ref[...], FIRST, preferred_element_type=F32)
    parcels, depth, _ = out_ref.shape
    unit = head_spread(heads, LANES, 1)
    tail = [
        lax.dot_general(part, unit, FIRST, preferred_element_type=F32)[0:1]
        for part in split2(jnp.broadcast_to(later, (heads, LANES)))
    ]
    out_ref[:, :, :width] = state_ref[...].astype(BF16).reshape(parcels, depth, width)
    tail = jnp.concatenate(tail, axis=0).astype(BF16)
    for k in range(parcels):
        out_ref[k, :, width:] = tail


def prefix_kernel(heads, in_ref, out_ref, log_ref):
    parcels, depth, width = out_ref.shape
    matrix = head_spread(LANES, width, width // heads)
    logs = in_ref[:, :, width:].reshape(parcels * depth, LANES)
    log_ref[...] = mm(logs, matrix)
    carried = jnp.zeros((depth, width), F32)
    for k in range(parcels):
        out_ref[k] = carried.astype(BF16)
        both = log_ref[k * depth : (k + 1) * depth, :]
        factor = jnp.exp(both[0:1, :] + both[1:2, :])
        carried = factor * carried + in_ref[k, :, :width].astype(F32)


def local_kernel(
    x_hbm,
    b_hbm,
    c_hbm,
    decay_hbm,
    skip_ref,
    out_ref,
    x_ref,
    b_ref,
    c_ref,
    decay_ref,
    state_ref,
    sems,
):
    copies = fetch(
        ((decay_hbm, decay_ref), (x_hbm, x_ref), (b_hbm, b_ref), (c_hbm, c_ref)), sems
    )
    heads, _, steps = decay_ref.shape
    width = x_ref.shape[1]
    matrix = head_spread(heads, width, width // heads)
    row = lax.broadcasted_iota(jnp.int32, (SPAN, SPAN), 0)
    column = lax.broadcasted_iota(jnp.int32, (SPAN, SPAN), 1)
    causal = row >= column
    first = lax.broadcasted_iota(jnp.int32, (heads, LANES), 1) < SPAN
    skip = sum(mm(part, matrix) for part in split3(skip_ref[...]))
    for copy in copies:
        copy.wait()
    before = jnp.zeros((heads, 1), F32)
    for k in range(steps // LANES):
        lanes = slice(k * LANES, (k + 1) * LANES)
        values = decay_ref[:, 0, lanes]
        reach = jnp.exp(running(values, lambda s, t: s <= t) + before)
        reach = jnp.concatenate([reach, jnp.zeros((ROWS - heads, LANES), F32)], axis=0)
        for part, half in enumerate(split2(reach)):
            out_ref[steps + part * ROWS : steps + (part + 1) * ROWS, lanes] = half
        before = before + jnp.sum(values, axis=1, keepdims=True)
        local = running(values, lambda s, t: (s <= t) & ((s < SPAN) == (t < SPAN)))
        middle = 0.5 * jnp.where(
            first, local[:, SPAN - 1 : SPAN], local[:, LANES - 1 : LANES]
        )
        ups = spread(jnp.exp(local - middle), matrix)
        downs = spread(jnp.exp(middle - local), matrix)
        for part in range(LANES // SPAN):
            inner = slice(part * SPAN, (part + 1) * SPAN)
            rows = slice(k * LANES + part * SPAN, k * LANES + (part + 1) * SPAN)
            up = ups[inner]
            half = up[SPAN - 1 : SPAN, :]
            x = x_ref[rows, :].astype(F32)
            b = b_ref[rows, :]
            c = c_ref[rows, :]
            scaled = (x * downs[inner]).astype(BF16)
            scores = lax.dot_general(c, b, LAST, preferred_element_type=F32)
            scores = jnp.where(causal, scores, 0.0).astype(BF16)
            y = mm(scores, scaled)
            update = lax.dot_general(b, scaled, FIRST, preferred_element_type=F32)
            if rows.start == 0:
                state_ref[...] = half * update
            else:
                state = state_ref[...]
                y = y + mm(c, (state * half).astype(BF16))
                state_ref[...] = half * (half * state + update)
            out_ref[rows, :width] = (up * y + skip * x).astype(BF16)
            out_ref[rows, width:] = c


def early_kernel(
    owners,
    capacity,
    w_hbm,
    local_hbm,
    routes_ref,
    gain_ref,
    w_ref,
    local_ref,
    target_ref,
    gain_out_ref,
    sems,
):
    copies = fetch(((w_hbm, w_ref), (local_hbm, local_ref)), sems)
    routes = routes_ref[...]
    rows = routes.shape[1]
    named = lax.broadcasted_iota(jnp.int32, (owners, rows), 0) == routes
    before = lax.broadcasted_iota(jnp.int32, (rows, rows), 0) < lax.broadcasted_iota(
        jnp.int32, (rows, rows), 1
    )
    earlier = mm(named.astype(BF16), before.astype(BF16))
    slot = jnp.sum(jnp.where(named, earlier, 0.0), axis=0, keepdims=True)
    target_ref[...] = routes * capacity + slot.astype(jnp.int32)
    gain_out_ref[...] = gain_ref[...]
    for copy in copies:
        copy.wait()


def project_kernel(heads, local_ref, prior_ref, w_ref, out_ref, mixed_ref):
    steps = mixed_ref.shape[0]
    parcels, depth, width = prior_ref.shape
    pieces, block, width_out = out_ref.shape
    state = prior_ref[...].reshape(parcels * depth, width)
    matrix = head_spread(ROWS, width, width // heads)
    for k in range(steps // LANES):
        rows = slice(k * LANES, (k + 1) * LANES)
        reach = sum(
            lax.dot_general(
                local_ref[steps + part * ROWS : steps + (part + 1) * ROWS, rows],
                matrix,
                FIRST,
                preferred_element_type=F32,
            )
            for part in range(2)
        )
        carried = reach * mm(local_ref[rows, width:], state)
        mixed_ref[rows, :] = (local_ref[rows, :width].astype(F32) + carried).astype(BF16)
    tile = 256
    for j in range(width_out // tile):
        columns = slice(j * tile, (j + 1) * tile)
        product = mm(mixed_ref[...], w_ref[:, columns]).astype(BF16)
        for d in range(pieces):
            out_ref[d, :, columns] = product[d * block : (d + 1) * block, :]


def regroup_kernel(target_ref, gain_ref, parts_ref, out_ref):
    owners, capacity, width = out_ref.shape
    pieces, rows, _ = parts_ref.shape
    projected = sum(parts_ref[k].astype(F32) for k in range(pieces))
    scale = lax.rsqrt(jnp.mean(projected * projected, axis=1, keepdims=True) + 1e-06)
    normed = (projected * scale * gain_ref[...]).astype(BF16)
    place = lax.broadcasted_iota(jnp.int32, (owners * capacity, rows), 0)
    select = (place == target_ref[...]).astype(BF16)
    out_ref[...] = mm(select, normed).astype(BF16).reshape(owners, capacity, width)


def call(kernel, outs, scratch, flops, moved, limit, *args, far=()):
    vmem = pl.BlockSpec(memory_space=pltpu.VMEM)
    hbm = pl.BlockSpec(memory_space=pltpu.HBM)
    return pl.pallas_call(
        kernel,
        out_shape=outs,
        in_specs=[hbm if k in far else vmem for k in range(len(args))],
        out_specs=jax.tree.map(lambda _: vmem, outs),
        scratch_shapes=scratch,
        cost_estimate=pl.CostEstimate(flops=flops, bytes_accessed=moved, transcendentals=0),
        compiler_params=pltpu.CompilerParams(vmem_limit_bytes=int(limit * 1024 * 1024)),
    )(*args)


def shards(head_inputs, b_proj, c_proj, log_decay, skip_gain, w_out, norm_gain, owner_ids):
    x, b, c, decays = head_inputs[0], b_proj[0], c_proj[0], log_decay.transpose(2, 0, 1)
    steps, width = x.shape
    heads = decays.shape[0]
    state_dim = b.shape[1]
    width_out = w_out.shape[1]
    times = lax.axis_size("tm")
    pieces = lax.axis_size("head")
    owners = times * lax.axis_size("farm")
    block = steps // pieces
    capacity = max(2, 2 * block // owners)
    depth = state_dim // times
    spec = jax.ShapeDtypeStruct
    wide = pltpu.VMEM((steps, width), BF16)
    narrow = pltpu.VMEM((steps, state_dim), BF16)
    state = pltpu.VMEM((state_dim, width), F32)
    parcel = call(
        state_kernel,
        spec((times, depth, width + LANES), BF16),
        [
            wide,
            narrow,
            pltpu.VMEM(decays.shape, F32),
            wide,
            state,
            pltpu.SemaphoreType.DMA((2 + steps // LANES,)),
        ],
        2 * steps * width * state_dim,
        2 * steps * width,
        63.4,
        x,
        b,
        decays,
        far=(0, 1, 2),
    )
    parcel = lax.all_to_all(parcel, "tm", split_axis=0, concat_axis=0, tiled=True)
    local = call(
        local_kernel,
        spec((steps + 2 * ROWS, width + state_dim), BF16),
        [
            wide,
            narrow,
            narrow,
            pltpu.VMEM(decays.shape, F32),
            state,
            pltpu.SemaphoreType.DMA((4,)),
        ],
        6 * steps * width * state_dim,
        8 * steps * width,
        61.5,
        x,
        b,
        c,
        decays,
        skip_gain[None, :],
        far=(0, 1, 2, 3),
    )
    parcel, local, w_late = lax.optimization_barrier((parcel, local, w_out))
    weights, local, target, gain = call(
        functools.partial(early_kernel, owners, capacity),
        (
            spec(w_out.shape, BF16),
            spec(local.shape, BF16),
            spec((1, block), jnp.int32),
            spec((1, width_out), F32),
        ),
        [pltpu.SemaphoreType.DMA((2,))],
        2 * owners * block * block,
        4 * width * width_out,
        16,
        w_late,
        local,
        owner_ids[0, :, 0][None, :],
        norm_gain[None, :],
        far=(0, 1),
    )
    prior = call(
        functools.partial(prefix_kernel, heads),
        spec((times, depth, width), BF16),
        [pltpu.VMEM((times * depth, width), F32)],
        2 * state_dim * width * LANES,
        4 * state_dim * width,
        16,
        parcel,
    )
    prior = lax.all_to_all(prior, "tm", split_axis=0, concat_axis=0, tiled=True)
    parts = call(
        functools.partial(project_kernel, heads),
        spec((pieces, block, width_out), BF16),
        [wide],
        2 * steps * width * (width_out + state_dim),
        2 * steps * (width + width_out) + 2 * width * width_out,
        24,
        local,
        prior,
        weights,
    )
    parts = lax.all_to_all(parts, "head", split_axis=0, concat_axis=0, tiled=True)
    outgoing = call(
        regroup_kernel,
        spec((owners, capacity, width_out), BF16),
        [],
        2 * owners * capacity * block * width_out,
        12 * block * width_out,
        16,
        target,
        gain,
        parts,
    )
    result = lax.all_to_all(outgoing, ("tm", "farm"), split_axis=0, concat_axis=0, tiled=True)
    return result[None, None]


def solution(mesh):
    placed = (
        P("farm", "tm", "head"),
        P("farm", "tm", None),
        P("farm", "tm", None),
        P("farm", "tm", "head"),
        P("head"),
        P("head", None),
        P(),
        P("farm", ("tm", "head"), None),
    )
    return jax.shard_map(
        shards,
        mesh=mesh,
        in_specs=placed,
        out_specs=P(("tm", "farm"), "head", None, None, None),
        check_vma=False,
    )
```

```python
import functools
import jax
import jax.numpy as jnp
from jax import lax
from jax.experimental import pallas as pl
from jax.experimental.pallas import tpu as pltpu
from jax.sharding import PartitionSpec as P

SPAN = 64
LANES = 128
ROWS = 16
TILE = 256
F32 = jnp.float32
BF16 = jnp.bfloat16
FIRST = (((0,), (0,)), ((), ()))
LAST = (((1,), (1,)), ((), ()))


def mm(a, b):
    return jnp.dot(a, b, preferred_element_type=F32)


def split2(value):
    high = value.astype(BF16)
    return high, (value - high.astype(F32)).astype(BF16)


def split3(value):
    high = value.astype(BF16)
    rest = value - high.astype(F32)
    middle = rest.astype(BF16)
    return high, middle, (rest - middle.astype(F32)).astype(BF16)


def head_spread(rows, width, group):
    head = lax.broadcasted_iota(jnp.int32, (rows, width), 0) * group
    lane = lax.broadcasted_iota(jnp.int32, (rows, width), 1)
    return ((lane >= head) & (lane < head + group)).astype(BF16)


def spread(value, matrix):
    high, low = split2(value)
    return lax.dot_general(high, matrix, FIRST, preferred_element_type=F32) + lax.dot_general(
        low, matrix, FIRST, preferred_element_type=F32
    )


def running(values, keep):
    length = values.shape[1]
    s = lax.broadcasted_iota(jnp.int32, (length, length), 0)
    t = lax.broadcasted_iota(jnp.int32, (length, length), 1)
    chosen = keep(s, t).astype(BF16)
    return sum(mm(part, chosen) for part in split3(values))


def fetch(pairs, sems):
    copies = [pltpu.make_async_copy(a, b, sems.at[i]) for i, (a, b) in enumerate(pairs)]
    for copy in copies:
        copy.start()
    return copies


def state_kernel(
    x_hbm, b_hbm, decay_hbm, out_ref, x_ref, b_ref, decay_ref, wx_ref, state_ref, sems
):
    heads, _, steps = decay_ref.shape
    width = x_ref.shape[1]
    blocks = [slice(k * LANES, (k + 1) * LANES) for k in range(steps // LANES)]
    first, *others, last = fetch(
        [(decay_hbm, decay_ref)]
        + [(x_hbm.at[rows, :], x_ref.at[rows, :]) for rows in blocks]
        + [(b_hbm, b_ref)],
        sems,
    )
    matrix = head_spread(heads, width, width // heads)
    later = jnp.zeros((heads, 1), F32)
    weights = [None] * len(blocks)
    first.wait()
    for k in reversed(range(len(blocks))):
        values = decay_ref[:, 0, blocks[k]]
        weights[k] = jnp.exp(running(values, lambda s, t: s > t) + later)
        later = later + jnp.sum(values, axis=1, keepdims=True)
    for rows, weight, copy in zip(blocks, weights, others):
        weight = spread(weight, matrix)
        copy.wait()
        wx_ref[rows, :] = (x_ref[rows, :].astype(F32) * weight).astype(BF16)
    last.wait()
    state_ref[...] = lax.dot_general(b_ref[...], wx_ref[...], FIRST, preferred_element_type=F32)
    parcels, depth, _ = out_ref.shape
    unit = head_spread(heads, LANES, 1)
    tail = [
        lax.dot_general(part, unit, FIRST, preferred_element_type=F32)[0:1]
        for part in split2(jnp.broadcast_to(later, (heads, LANES)))
    ]
    out_ref[:, :, :width] = state_ref[...].astype(BF16).reshape(parcels, depth, width)
    tail = jnp.concatenate(tail, axis=0).astype(BF16)
    for k in range(parcels):
        out_ref[k, :, width:] = tail


def prefix_kernel(heads, in_ref, out_ref, log_ref):
    parcels, depth, width = out_ref.shape
    matrix = head_spread(LANES, width, width // heads)
    logs = in_ref[:, :, width:].reshape(parcels * depth, LANES)
    log_ref[...] = mm(logs, matrix)
    carried = jnp.zeros((depth, width), F32)
    for k in range(parcels):
        out_ref[k] = carried.astype(BF16)
        both = log_ref[k * depth : (k + 1) * depth, :]
        factor = jnp.exp(both[0:1, :] + both[1:2, :])
        carried = factor * carried + in_ref[k, :, :width].astype(F32)


def local_kernel(
    x_hbm,
    b_hbm,
    c_hbm,
    decay_hbm,
    skip_ref,
    out_ref,
    x_ref,
    b_ref,
    c_ref,
    decay_ref,
    state_ref,
    sems,
):
    copies = fetch(
        ((decay_hbm, decay_ref), (x_hbm, x_ref), (b_hbm, b_ref), (c_hbm, c_ref)), sems
    )
    heads, _, steps = decay_ref.shape
    width = x_ref.shape[1]
    matrix = head_spread(heads, width, width // heads)
    row = lax.broadcasted_iota(jnp.int32, (SPAN, SPAN), 0)
    column = lax.broadcasted_iota(jnp.int32, (SPAN, SPAN), 1)
    causal = row >= column
    first = lax.broadcasted_iota(jnp.int32, (heads, LANES), 1) < SPAN
    skip = sum(mm(part, matrix) for part in split3(skip_ref[...]))
    for copy in copies:
        copy.wait()
    before = jnp.zeros((heads, 1), F32)
    for k in range(steps // LANES):
        lanes = slice(k * LANES, (k + 1) * LANES)
        values = decay_ref[:, 0, lanes]
        reach = jnp.exp(running(values, lambda s, t: s <= t) + before)
        reach = jnp.concatenate([reach, jnp.zeros((ROWS - heads, LANES), F32)], axis=0)
        for part, half in enumerate(split2(reach)):
            out_ref[steps + part * ROWS : steps + (part + 1) * ROWS, lanes] = half
        before = before + jnp.sum(values, axis=1, keepdims=True)
        local = running(values, lambda s, t: (s <= t) & ((s < SPAN) == (t < SPAN)))
        middle = 0.5 * jnp.where(
            first, local[:, SPAN - 1 : SPAN], local[:, LANES - 1 : LANES]
        )
        ups = spread(jnp.exp(local - middle), matrix)
        downs = spread(jnp.exp(middle - local), matrix)
        for part in range(LANES // SPAN):
            inner = slice(part * SPAN, (part + 1) * SPAN)
            rows = slice(k * LANES + part * SPAN, k * LANES + (part + 1) * SPAN)
            up = ups[inner]
            half = up[SPAN - 1 : SPAN, :]
            x = x_ref[rows, :].astype(F32)
            b = b_ref[rows, :]
            c = c_ref[rows, :]
            scaled = (x * downs[inner]).astype(BF16)
            scores = lax.dot_general(c, b, LAST, preferred_element_type=F32)
            scores = jnp.where(causal, scores, 0.0).astype(BF16)
            y = mm(scores, scaled)
            update = lax.dot_general(b, scaled, FIRST, preferred_element_type=F32)
            if rows.start == 0:
                state_ref[...] = half * update
            else:
                state = state_ref[...]
                y = y + mm(c, (state * half).astype(BF16))
                state_ref[...] = half * (half * state + update)
            out_ref[rows, :width] = (up * y + skip * x).astype(BF16)
            out_ref[rows, width:] = c


def early_kernel(
    owners,
    capacity,
    local_hbm,
    routes_ref,
    gain_ref,
    local_ref,
    target_ref,
    gain_out_ref,
    sems,
):
    copies = fetch(((local_hbm, local_ref),), sems)
    routes = routes_ref[...]
    rows = routes.shape[1]
    named = lax.broadcasted_iota(jnp.int32, (owners, rows), 0) == routes
    before = lax.broadcasted_iota(jnp.int32, (rows, rows), 0) < lax.broadcasted_iota(
        jnp.int32, (rows, rows), 1
    )
    earlier = mm(named.astype(BF16), before.astype(BF16))
    slot = jnp.sum(jnp.where(named, earlier, 0.0), axis=0, keepdims=True)
    target_ref[...] = routes * capacity + slot.astype(jnp.int32)
    gain_out_ref[...] = gain_ref[...]
    for copy in copies:
        copy.wait()


def project_kernel(heads, index_ref, local_ref, prior_ref, w_ref, *rest):
    outs, mixed_ref = rest[:-1], rest[-1]
    tiles = [slice(k, k + TILE) for k in range(0, w_ref.shape[1], TILE)]
    steps = mixed_ref.shape[0]
    parcels, depth, width = prior_ref.shape
    pieces = len(outs)
    block, width_out = outs[0].shape
    state = prior_ref[...].reshape(parcels * depth, width)
    matrix = head_spread(ROWS, width, width // heads)
    for k in range(pieces):
        rows = slice(k * block, (k + 1) * block)
        reach = sum(
            lax.dot_general(
                local_ref[steps + part * ROWS : steps + (part + 1) * ROWS, rows],
                matrix,
                FIRST,
                preferred_element_type=F32,
            )
            for part in range(2)
        )
        carried = reach * mm(local_ref[rows, width:], state)
        ahead = lax.rem(k - index_ref[0] + pieces, pieces)
        mixed_ref[pl.ds(pl.multiple_of(ahead * block, block), block), :] = (
            local_ref[rows, :width].astype(F32) + carried
        ).astype(BF16)
    for columns in tiles:
        product = mm(mixed_ref[...], w_ref[:, columns]).astype(BF16)
        for d in range(pieces):
            outs[d][:, columns] = product[d * block : (d + 1) * block, :]


def regroup_kernel(target_ref, gain_ref, *rest):
    parts, out_ref = rest[:-1], rest[-1]
    owners, capacity, width = out_ref.shape
    rows = parts[0].shape[0]
    projected = sum(part[...].astype(F32) for part in parts)
    scale = lax.rsqrt(jnp.mean(projected * projected, axis=1, keepdims=True) + 1e-06)
    normed = (projected * scale * gain_ref[...]).astype(BF16)
    place = lax.broadcasted_iota(jnp.int32, (owners * capacity, rows), 0)
    select = (place == target_ref[...]).astype(BF16)
    out_ref[...] = mm(select, normed).astype(BF16).reshape(owners, capacity, width)


def call(kernel, outs, scratch, flops, moved, limit, *args, far=(), scalars=()):
    vmem = pl.BlockSpec(memory_space=pltpu.VMEM)
    hbm = pl.BlockSpec(memory_space=pltpu.HBM)
    smem = pl.BlockSpec(memory_space=pltpu.SMEM)
    return pl.pallas_call(
        kernel,
        out_shape=outs,
        in_specs=[hbm if k in far else smem if k in scalars else vmem for k in range(len(args))],
        out_specs=jax.tree.map(lambda _: vmem, outs),
        scratch_shapes=scratch,
        cost_estimate=pl.CostEstimate(flops=flops, bytes_accessed=moved, transcendentals=0),
        compiler_params=pltpu.CompilerParams(vmem_limit_bytes=int(limit * 1024 * 1024)),
    )(*args)


def shards(head_inputs, b_proj, c_proj, log_decay, skip_gain, w_out, norm_gain, owner_ids):
    x, b, c, decays = head_inputs[0], b_proj[0], c_proj[0], log_decay.transpose(2, 0, 1)
    steps, width = x.shape
    heads = decays.shape[0]
    state_dim = b.shape[1]
    width_out = w_out.shape[1]
    times = lax.axis_size("tm")
    pieces = lax.axis_size("head")
    owners = times * lax.axis_size("farm")
    block = steps // pieces
    capacity = max(2, 2 * block // owners)
    depth = state_dim // times
    spec = jax.ShapeDtypeStruct
    wide = pltpu.VMEM((steps, width), BF16)
    narrow = pltpu.VMEM((steps, state_dim), BF16)
    state = pltpu.VMEM((state_dim, width), F32)
    parcel = call(
        state_kernel,
        spec((times, depth, width + LANES), BF16),
        [
            wide,
            narrow,
            pltpu.VMEM(decays.shape, F32),
            wide,
            state,
            pltpu.SemaphoreType.DMA((2 + steps // LANES,)),
        ],
        2 * steps * width * state_dim,
        2 * steps * width,
        63.4,
        x,
        b,
        decays,
        far=(0, 1, 2),
    )
    parcel = lax.all_to_all(parcel, "tm", split_axis=0, concat_axis=0, tiled=True)
    local = call(
        local_kernel,
        spec((steps + 2 * ROWS, width + state_dim), BF16),
        [
            wide,
            narrow,
            narrow,
            pltpu.VMEM(decays.shape, F32),
            state,
            pltpu.SemaphoreType.DMA((4,)),
        ],
        6 * steps * width * state_dim,
        8 * steps * width,
        61.5,
        x,
        b,
        c,
        decays,
        skip_gain[None, :],
        far=(0, 1, 2, 3),
    )
    parcel, local = lax.optimization_barrier((parcel, local))
    local, target, gain = call(
        functools.partial(early_kernel, owners, capacity),
        (
            spec(local.shape, BF16),
            spec((1, block), jnp.int32),
            spec((1, width_out), F32),
        ),
        [pltpu.SemaphoreType.DMA((1,))],
        2 * owners * block * block,
        4 * steps * width,
        16,
        local,
        owner_ids[0, :, 0][None, :],
        norm_gain[None, :],
        far=(0,),
    )
    prior = call(
        functools.partial(prefix_kernel, heads),
        spec((times, depth, width), BF16),
        [pltpu.VMEM((times * depth, width), F32)],
        2 * state_dim * width * LANES,
        4 * state_dim * width,
        16,
        parcel,
    )
    prior = lax.all_to_all(prior, "tm", split_axis=0, concat_axis=0, tiled=True)
    index = lax.axis_index("head").astype(jnp.int32).reshape(1)
    parts = call(
        functools.partial(project_kernel, heads),
        (spec((block, width_out), BF16),) * pieces,
        [wide],
        2 * steps * width * (width_out + state_dim),
        2 * steps * (width + width_out) + 2 * width * width_out,
        24,
        index,
        local,
        prior,
        w_out,
        scalars=(0,),
    )
    ring = range(pieces)
    moved = [
        lax.ppermute(parts[d], "head", [(k, (k + d) % pieces) for k in ring]) for d in (2, 1, 3)
    ]
    outgoing = call(
        regroup_kernel,
        spec((owners, capacity, width_out), BF16),
        [],
        2 * owners * capacity * block * width_out,
        12 * block * width_out,
        16,
        target,
        gain,
        parts[0],
        *moved,
    )
    result = lax.all_to_all(outgoing, ("tm", "farm"), split_axis=0, concat_axis=0, tiled=True)
    return result[None, None]


def solution(mesh):
    placed = (
        P("farm", "tm", "head"),
        P("farm", "tm", None),
        P("farm", "tm", None),
        P("farm", "tm", "head"),
        P("head"),
        P("head", None),
        P(),
        P("farm", ("tm", "head"), None),
    )
    return jax.shard_map(
        shards,
        mesh=mesh,
        in_specs=placed,
        out_specs=P(("tm", "farm"), "head", None, None, None),
        check_vma=False,
    )
```

```python
import functools
import jax
import jax.numpy as jnp
from jax import lax
from jax.experimental import pallas as pl
from jax.experimental.pallas import tpu as pltpu
from jax.sharding import PartitionSpec as P

SPAN = 64
LANES = 128
ROWS = 16
SHELF = 12288
TILE = 256
F32 = jnp.float32
BF16 = jnp.bfloat16
FIRST = (((0,), (0,)), ((), ()))
LAST = (((1,), (1,)), ((), ()))


def mm(a, b):
    return jnp.dot(a, b, preferred_element_type=F32)


def split2(value):
    high = value.astype(BF16)
    return high, (value - high.astype(F32)).astype(BF16)


def split3(value):
    high = value.astype(BF16)
    rest = value - high.astype(F32)
    middle = rest.astype(BF16)
    return high, middle, (rest - middle.astype(F32)).astype(BF16)


def head_spread(rows, width, group):
    head = lax.broadcasted_iota(jnp.int32, (rows, width), 0) * group
    lane = lax.broadcasted_iota(jnp.int32, (rows, width), 1)
    return ((lane >= head) & (lane < head + group)).astype(BF16)


def spread(value, matrix):
    high, low = split2(value)
    return lax.dot_general(high, matrix, FIRST, preferred_element_type=F32) + lax.dot_general(
        low, matrix, FIRST, preferred_element_type=F32
    )


def running(values, keep):
    length = values.shape[1]
    s = lax.broadcasted_iota(jnp.int32, (length, length), 0)
    t = lax.broadcasted_iota(jnp.int32, (length, length), 1)
    chosen = keep(s, t).astype(BF16)
    return sum(mm(part, chosen) for part in split3(values))


def fetch(pairs, sems):
    copies = [pltpu.make_async_copy(a, b, sems.at[i]) for i, (a, b) in enumerate(pairs)]
    for copy in copies:
        copy.start()
    return copies


def state_kernel(
    x_hbm, b_hbm, decay_hbm, out_ref, x_ref, b_ref, decay_ref, wx_ref, state_ref, sems
):
    heads, _, steps = decay_ref.shape
    width = x_ref.shape[1]
    blocks = [slice(k * LANES, (k + 1) * LANES) for k in range(steps // LANES)]
    first, second, *others = fetch(
        [(decay_hbm, decay_ref), (b_hbm, b_ref)]
        + [(x_hbm.at[rows, :], x_ref.at[rows, :]) for rows in blocks],
        sems,
    )
    matrix = head_spread(heads, width, width // heads)
    later = jnp.zeros((heads, 1), F32)
    weights = [None] * len(blocks)
    first.wait()
    for k in reversed(range(len(blocks))):
        values = decay_ref[:, 0, blocks[k]]
        weights[k] = jnp.exp(running(values, lambda s, t: s > t) + later)
        later = later + jnp.sum(values, axis=1, keepdims=True)
    second.wait()
    across = b_ref[...].T
    for rows, weight, copy in zip(blocks, weights, others):
        weight = spread(weight, matrix)
        copy.wait()
        wx_ref[rows, :] = (x_ref[rows, :].astype(F32) * weight).astype(BF16)
    state_ref[...] = mm(across, wx_ref[...])
    parcels, depth, _ = out_ref.shape
    unit = head_spread(heads, LANES, 1)
    tail = [
        lax.dot_general(part, unit, FIRST, preferred_element_type=F32)[0:1]
        for part in split2(jnp.broadcast_to(later, (heads, LANES)))
    ]
    out_ref[:, :, :width] = state_ref[...].astype(BF16).reshape(parcels, depth, width)
    tail = jnp.concatenate(tail, axis=0).astype(BF16)
    for k in range(parcels):
        out_ref[k, :, width:] = tail


def prefix_kernel(heads, in_ref, out_ref, factor_ref):
    parcels, depth, width = out_ref.shape
    matrix = head_spread(LANES, width, width // heads)
    pairs = head_spread(parcels, parcels * depth, depth)
    logs = mm(pairs, in_ref[:, :, width:].reshape(parcels * depth, LANES))
    factor_ref[...] = sum(mm(part, matrix) for part in split2(jnp.exp(logs)))
    carried = jnp.zeros((depth, width), F32)
    for k in range(parcels):
        out_ref[k] = carried.astype(BF16)
        carried = factor_ref[k : k + 1, :] * carried + in_ref[k, :, :width].astype(F32)


def local_kernel(
    x_hbm,
    b_hbm,
    c_hbm,
    decay_hbm,
    skip_ref,
    out_ref,
    x_ref,
    b_ref,
    c_ref,
    decay_ref,
    state_ref,
    sems,
):
    copies = fetch(
        ((decay_hbm, decay_ref), (x_hbm, x_ref), (b_hbm, b_ref), (c_hbm, c_ref)), sems
    )
    heads, _, steps = decay_ref.shape
    width = x_ref.shape[1]
    matrix = head_spread(heads, width, width // heads)
    row = lax.broadcasted_iota(jnp.int32, (SPAN, SPAN), 0)
    column = lax.broadcasted_iota(jnp.int32, (SPAN, SPAN), 1)
    causal = row >= column
    first = lax.broadcasted_iota(jnp.int32, (heads, LANES), 1) < SPAN
    skip = sum(mm(part, matrix) for part in split3(skip_ref[...]))
    for copy in copies:
        copy.wait()
    before = jnp.zeros((heads, 1), F32)
    for k in range(steps // LANES):
        lanes = slice(k * LANES, (k + 1) * LANES)
        values = decay_ref[:, 0, lanes]
        reach = jnp.exp(running(values, lambda s, t: s <= t) + before)
        reach = jnp.concatenate([reach, jnp.zeros((ROWS - heads, LANES), F32)], axis=0)
        for part, half in enumerate(split2(reach)):
            out_ref[steps + part * ROWS : steps + (part + 1) * ROWS, lanes] = half
        before = before + jnp.sum(values, axis=1, keepdims=True)
        local = running(values, lambda s, t: (s <= t) & ((s < SPAN) == (t < SPAN)))
        middle = 0.5 * jnp.where(
            first, local[:, SPAN - 1 : SPAN], local[:, LANES - 1 : LANES]
        )
        ups = spread(jnp.exp(local - middle), matrix)
        downs = spread(jnp.exp(middle - local), matrix)
        for part in range(LANES // SPAN):
            inner = slice(part * SPAN, (part + 1) * SPAN)
            rows = slice(k * LANES + part * SPAN, k * LANES + (part + 1) * SPAN)
            up = ups[inner]
            half = up[SPAN - 1 : SPAN, :]
            x = x_ref[rows, :].astype(F32)
            b = b_ref[rows, :]
            c = c_ref[rows, :]
            scaled = (x * downs[inner]).astype(BF16)
            scores = lax.dot_general(c, b, LAST, preferred_element_type=F32)
            scores = jnp.where(causal, scores, 0.0).astype(BF16)
            y = mm(scores, scaled)
            update = lax.dot_general(b, scaled, FIRST, preferred_element_type=F32)
            if rows.start == 0:
                state_ref[...] = half * update
            else:
                state = state_ref[...]
                y = y + mm(c, (state * half).astype(BF16))
                state_ref[...] = half * (half * state + update)
            out_ref[rows, :width] = (up * y + skip * x).astype(BF16)
            out_ref[rows, width:] = c


def early_kernel(
    owners,
    capacity,
    local_hbm,
    w_hbm,
    routes_ref,
    gain_ref,
    local_ref,
    shelf_hbm,
    target_ref,
    gain_out_ref,
    sems,
):
    depth, width_out = w_hbm.shape
    copies = fetch(
        ((local_hbm, local_ref), (w_hbm, shelf_hbm.at[pl.ds(0, depth), :])), sems
    )
    routes = routes_ref[...]
    rows = routes.shape[1]
    named = lax.broadcasted_iota(jnp.int32, (owners, rows), 0) == routes
    before = lax.broadcasted_iota(jnp.int32, (rows, rows), 0) < lax.broadcasted_iota(
        jnp.int32, (rows, rows), 1
    )
    earlier = mm(named.astype(BF16), before.astype(BF16))
    slot = jnp.sum(jnp.where(named, earlier, 0.0), axis=0, keepdims=True)
    target_ref[...] = routes * capacity + slot.astype(jnp.int32)
    gain_out_ref[...] = gain_ref[...]
    for copy in copies:
        copy.wait()


def project_kernel(heads, index_ref, local_ref, prior_ref, w_hbm, *rest):
    outs, (mixed_ref, w_ref, sems) = rest[:-3], rest[-3:]
    tiles = [slice(k, k + TILE) for k in range(0, w_ref.shape[1], TILE)]
    taken = pl.ds(0, w_ref.shape[0])
    copies = fetch([(w_hbm.at[taken, lanes], w_ref.at[:, lanes]) for lanes in tiles], sems)
    steps = mixed_ref.shape[0]
    parcels, depth, width = prior_ref.shape
    pieces = len(outs)
    block, width_out = outs[0].shape
    state = prior_ref[...].reshape(parcels * depth, width)
    matrix = head_spread(ROWS, width, width // heads)
    for k in range(pieces):
        rows = slice(k * block, (k + 1) * block)
        reach = sum(
            lax.dot_general(
                local_ref[steps + part * ROWS : steps + (part + 1) * ROWS, rows],
                matrix,
                FIRST,
                preferred_element_type=F32,
            )
            for part in range(2)
        )
        carried = reach * mm(local_ref[rows, width:], state)
        ahead = lax.rem(k - index_ref[0] + pieces, pieces)
        mixed_ref[pl.ds(pl.multiple_of(ahead * block, block), block), :] = (
            local_ref[rows, :width].astype(F32) + carried
        ).astype(BF16)
    for columns, copy in zip(tiles, copies):
        copy.wait()
        product = mm(mixed_ref[...], w_ref[:, columns]).astype(BF16)
        for d in range(pieces):
            outs[d][:, columns] = product[d * block : (d + 1) * block, :]


def regroup_kernel(target_ref, gain_ref, *rest):
    parts, out_ref = rest[:-1], rest[-1]
    owners, capacity, width = out_ref.shape
    rows = parts[0].shape[0]
    projected = sum(part[...].astype(F32) for part in parts)
    scale = lax.rsqrt(jnp.mean(projected * projected, axis=1, keepdims=True) + 1e-06)
    normed = (projected * scale * gain_ref[...]).astype(BF16)
    place = lax.broadcasted_iota(jnp.int32, (owners * capacity, rows), 0)
    select = (place == target_ref[...]).astype(BF16)
    out_ref[...] = mm(select, normed).astype(BF16).reshape(owners, capacity, width)


def call(kernel, outs, scratch, flops, moved, limit, *args, far=(), far_out=(), scalars=()):
    vmem = pl.BlockSpec(memory_space=pltpu.VMEM)
    hbm = pl.BlockSpec(memory_space=pltpu.HBM)
    smem = pl.BlockSpec(memory_space=pltpu.SMEM)
    return pl.pallas_call(
        kernel,
        out_shape=outs,
        in_specs=[hbm if k in far else smem if k in scalars else vmem for k in range(len(args))],
        out_specs=tuple(hbm if k in far_out else vmem for k in range(len(outs)))
        if isinstance(outs, tuple)
        else vmem,
        scratch_shapes=scratch,
        cost_estimate=pl.CostEstimate(flops=flops, bytes_accessed=moved, transcendentals=0),
        compiler_params=pltpu.CompilerParams(vmem_limit_bytes=int(limit * 1024 * 1024)),
    )(*args)


def shards(head_inputs, b_proj, c_proj, log_decay, skip_gain, w_out, norm_gain, owner_ids):
    x, b, c, decays = head_inputs[0], b_proj[0], c_proj[0], log_decay.transpose(2, 0, 1)
    steps, width = x.shape
    heads = decays.shape[0]
    state_dim = b.shape[1]
    width_out = w_out.shape[1]
    times = lax.axis_size("tm")
    pieces = lax.axis_size("head")
    owners = times * lax.axis_size("farm")
    block = steps // pieces
    capacity = max(2, 2 * block // owners)
    depth = state_dim // times
    spec = jax.ShapeDtypeStruct
    wide = pltpu.VMEM((steps, width), BF16)
    narrow = pltpu.VMEM((steps, state_dim), BF16)
    state = pltpu.VMEM((state_dim, width), F32)
    parcel = call(
        state_kernel,
        spec((times, depth, width + LANES), BF16),
        [
            wide,
            narrow,
            pltpu.VMEM(decays.shape, F32),
            wide,
            state,
            pltpu.SemaphoreType.DMA((2 + steps // LANES,)),
        ],
        2 * steps * width * state_dim,
        2 * steps * width,
        63.4,
        x,
        b,
        decays,
        far=(0, 1, 2),
    )
    parcel = lax.all_to_all(parcel, "tm", split_axis=0, concat_axis=0, tiled=True)
    local = call(
        local_kernel,
        spec((steps + 2 * ROWS, width + state_dim), BF16),
        [
            wide,
            narrow,
            narrow,
            pltpu.VMEM(decays.shape, F32),
            state,
            pltpu.SemaphoreType.DMA((4,)),
        ],
        6 * steps * width * state_dim,
        8 * steps * width,
        61.5,
        x,
        b,
        c,
        decays,
        skip_gain[None, :],
        far=(0, 1, 2, 3),
    )
    parcel, local, w_late = lax.optimization_barrier((parcel, local, w_out))
    local, shelf, target, gain = call(
        functools.partial(early_kernel, owners, capacity),
        (
            spec(local.shape, BF16),
            spec((SHELF, width_out), BF16),
            spec((1, block), jnp.int32),
            spec((1, width_out), F32),
        ),
        [pltpu.SemaphoreType.DMA((2,))],
        2 * owners * block * block,
        4 * width * width_out,
        16,
        local,
        w_late,
        owner_ids[0, :, 0][None, :],
        norm_gain[None, :],
        far=(0, 1),
        far_out=(1,),
    )
    prior = call(
        functools.partial(prefix_kernel, heads),
        spec((times, depth, width), BF16),
        [pltpu.VMEM((times, width), F32)],
        2 * state_dim * width * LANES,
        4 * state_dim * width,
        16,
        parcel,
    )
    prior = lax.all_to_all(prior, "tm", split_axis=0, concat_axis=0, tiled=True)
    index = lax.axis_index("head").astype(jnp.int32).reshape(1)
    parts = call(
        functools.partial(project_kernel, heads),
        (spec((block, width_out), BF16),) * pieces,
        [
            wide,
            pltpu.VMEM(w_out.shape, BF16),
            pltpu.SemaphoreType.DMA((width_out // TILE,)),
        ],
        2 * steps * width * (width_out + state_dim),
        2 * steps * (width + width_out) + 2 * width * width_out,
        40,
        index,
        local,
        prior,
        shelf,
        far=(3,),
        scalars=(0,),
    )
    ring = range(pieces)
    moved = [
        lax.ppermute(parts[d], "head", [(k, (k + d) % pieces) for k in ring]) for d in (2, 1, 3)
    ]
    outgoing = call(
        regroup_kernel,
        spec((owners, capacity, width_out), BF16),
        [],
        2 * owners * capacity * block * width_out,
        12 * block * width_out,
        16,
        target,
        gain,
        parts[0],
        *moved,
    )
    result = lax.all_to_all(outgoing, ("tm", "farm"), split_axis=0, concat_axis=0, tiled=True)
    return result[None, None]


def solution(mesh):
    placed = (
        P("farm", "tm", "head"),
        P("farm", "tm", None),
        P("farm", "tm", None),
        P("farm", "tm", "head"),
        P("head"),
        P("head", None),
        P(),
        P("farm", ("tm", "head"), None),
    )
    return jax.shard_map(
        shards,
        mesh=mesh,
        in_specs=placed,
        out_specs=P(("tm", "farm"), "head", None, None, None),
        check_vma=False,
    )
```

```python
import functools
import jax
import jax.numpy as jnp
from jax import lax
from jax.experimental import pallas as pl
from jax.experimental.pallas import tpu as pltpu
from jax.sharding import PartitionSpec as P

SPAN = 64
LANES = 128
ROWS = 16
F32 = jnp.float32
BF16 = jnp.bfloat16
FIRST = (((0,), (0,)), ((), ()))
LAST = (((1,), (1,)), ((), ()))


def mm(a, b):
    return jnp.dot(a, b, preferred_element_type=F32)


def split2(value):
    high = value.astype(BF16)
    return high, (value - high.astype(F32)).astype(BF16)


def split3(value):
    high = value.astype(BF16)
    rest = value - high.astype(F32)
    middle = rest.astype(BF16)
    return high, middle, (rest - middle.astype(F32)).astype(BF16)


def head_spread(rows, width, group):
    head = lax.broadcasted_iota(jnp.int32, (rows, width), 0) * group
    lane = lax.broadcasted_iota(jnp.int32, (rows, width), 1)
    return ((lane >= head) & (lane < head + group)).astype(BF16)


def spread(value, matrix):
    high, low = split2(value)
    return lax.dot_general(high, matrix, FIRST, preferred_element_type=F32) + lax.dot_general(
        low, matrix, FIRST, preferred_element_type=F32
    )


def running(values, keep):
    length = values.shape[1]
    s = lax.broadcasted_iota(jnp.int32, (length, length), 0)
    t = lax.broadcasted_iota(jnp.int32, (length, length), 1)
    chosen = keep(s, t).astype(BF16)
    return sum(mm(part, chosen) for part in split3(values))


def fetch(pairs, sems):
    copies = [pltpu.make_async_copy(a, b, sems.at[i]) for i, (a, b) in enumerate(pairs)]
    for copy in copies:
        copy.start()
    return copies


def state_kernel(
    x_hbm, b_hbm, decay_hbm, out_ref, x_ref, b_ref, decay_ref, wx_ref, state_ref, sems
):
    heads, _, steps = decay_ref.shape
    width = x_ref.shape[1]
    blocks = [slice(k * LANES, (k + 1) * LANES) for k in range(steps // LANES)]
    first, *others, last = fetch(
        [(decay_hbm, decay_ref)]
        + [(x_hbm.at[rows, :], x_ref.at[rows, :]) for rows in blocks]
        + [(b_hbm, b_ref)],
        sems,
    )
    matrix = head_spread(heads, width, width // heads)
    later = jnp.zeros((heads, 1), F32)
    weights = [None] * len(blocks)
    first.wait()
    for k in reversed(range(len(blocks))):
        values = decay_ref[:, 0, blocks[k]]
        weights[k] = jnp.exp(running(values, lambda s, t: s > t) + later)
        later = later + jnp.sum(values, axis=1, keepdims=True)
    for rows, weight, copy in zip(blocks, weights, others):
        weight = spread(weight, matrix)
        copy.wait()
        wx_ref[rows, :] = (x_ref[rows, :].astype(F32) * weight).astype(BF16)
    last.wait()
    state_ref[...] = lax.dot_general(b_ref[...], wx_ref[...], FIRST, preferred_element_type=F32)
    parcels, depth, _ = out_ref.shape
    unit = head_spread(heads, LANES, 1)
    tail = [
        lax.dot_general(part, unit, FIRST, preferred_element_type=F32)[0:1]
        for part in split2(jnp.broadcast_to(later, (heads, LANES)))
    ]
    out_ref[:, :, :width] = state_ref[...].astype(BF16).reshape(parcels, depth, width)
    tail = jnp.concatenate(tail, axis=0).astype(BF16)
    for k in range(parcels):
        out_ref[k, :, width:] = tail


def prefix_kernel(heads, in_ref, out_ref, log_ref):
    parcels, depth, width = out_ref.shape
    matrix = head_spread(LANES, width, width // heads)
    logs = in_ref[:, :, width:].reshape(parcels * depth, LANES)
    log_ref[...] = mm(logs, matrix)
    carried = jnp.zeros((depth, width), F32)
    for k in range(parcels):
        out_ref[k] = carried.astype(BF16)
        both = log_ref[k * depth : (k + 1) * depth, :]
        factor = jnp.exp(both[0:1, :] + both[1:2, :])
        carried = factor * carried + in_ref[k, :, :width].astype(F32)


def local_kernel(
    x_hbm,
    b_hbm,
    c_hbm,
    decay_hbm,
    skip_ref,
    out_ref,
    x_ref,
    b_ref,
    c_ref,
    decay_ref,
    state_ref,
    sems,
):
    copies = fetch(
        ((decay_hbm, decay_ref), (x_hbm, x_ref), (b_hbm, b_ref), (c_hbm, c_ref)), sems
    )
    heads, _, steps = decay_ref.shape
    width = x_ref.shape[1]
    matrix = head_spread(heads, width, width // heads)
    row = lax.broadcasted_iota(jnp.int32, (SPAN, SPAN), 0)
    column = lax.broadcasted_iota(jnp.int32, (SPAN, SPAN), 1)
    causal = row >= column
    first = lax.broadcasted_iota(jnp.int32, (heads, LANES), 1) < SPAN
    skip = sum(mm(part, matrix) for part in split3(skip_ref[...]))
    for copy in copies:
        copy.wait()
    before = jnp.zeros((heads, 1), F32)
    for k in range(steps // LANES):
        lanes = slice(k * LANES, (k + 1) * LANES)
        values = decay_ref[:, 0, lanes]
        reach = jnp.exp(running(values, lambda s, t: s <= t) + before)
        reach = jnp.concatenate([reach, jnp.zeros((ROWS - heads, LANES), F32)], axis=0)
        for part, half in enumerate(split2(reach)):
            out_ref[steps + part * ROWS : steps + (part + 1) * ROWS, lanes] = half
        before = before + jnp.sum(values, axis=1, keepdims=True)
        local = running(values, lambda s, t: (s <= t) & ((s < SPAN) == (t < SPAN)))
        middle = 0.5 * jnp.where(
            first, local[:, SPAN - 1 : SPAN], local[:, LANES - 1 : LANES]
        )
        ups = spread(jnp.exp(local - middle), matrix)
        downs = spread(jnp.exp(middle - local), matrix)
        for part in range(LANES // SPAN):
            inner = slice(part * SPAN, (part + 1) * SPAN)
            rows = slice(k * LANES + part * SPAN, k * LANES + (part + 1) * SPAN)
            up = ups[inner]
            half = up[SPAN - 1 : SPAN, :]
            x = x_ref[rows, :].astype(F32)
            b = b_ref[rows, :]
            c = c_ref[rows, :]
            scaled = (x * downs[inner]).astype(BF16)
            scores = lax.dot_general(c, b, LAST, preferred_element_type=F32)
            scores = jnp.where(causal, scores, 0.0).astype(BF16)
            y = mm(scores, scaled)
            update = lax.dot_general(b, scaled, FIRST, preferred_element_type=F32)
            if rows.start == 0:
                state_ref[...] = half * update
            else:
                state = state_ref[...]
                y = y + mm(c, (state * half).astype(BF16))
                state_ref[...] = half * (half * state + update)
            out_ref[rows, :width] = (up * y + skip * x).astype(BF16)
            out_ref[rows, width:] = c


def early_kernel(
    owners,
    capacity,
    w_hbm,
    local_hbm,
    routes_ref,
    gain_ref,
    w_ref,
    local_ref,
    target_ref,
    gain_out_ref,
    token_ref,
    sems,
):
    copies = fetch(((w_hbm, w_ref), (local_hbm, local_ref)), sems)
    routes = routes_ref[...]
    rows = routes.shape[1]
    named = lax.broadcasted_iota(jnp.int32, (owners, rows), 0) == routes
    before = lax.broadcasted_iota(jnp.int32, (rows, rows), 0) < lax.broadcasted_iota(
        jnp.int32, (rows, rows), 1
    )
    earlier = mm(named.astype(BF16), before.astype(BF16))
    slot = jnp.sum(jnp.where(named, earlier, 0.0), axis=0, keepdims=True)
    target_ref[...] = routes * capacity + slot.astype(jnp.int32)
    gain_out_ref[...] = gain_ref[...]
    token_ref[...] = jnp.zeros(token_ref.shape, BF16)
    for copy in copies:
        copy.wait()


def project_kernel(heads, local_ref, prior_ref, w_ref, token_ref, out_ref, mixed_ref):
    steps = mixed_ref.shape[0]
    parcels, depth, width = prior_ref.shape
    pieces, block, width_out = out_ref.shape
    state = prior_ref[...].reshape(parcels * depth, width)
    matrix = head_spread(ROWS, width, width // heads)
    for k in range(steps // LANES):
        rows = slice(k * LANES, (k + 1) * LANES)
        reach = sum(
            lax.dot_general(
                local_ref[steps + part * ROWS : steps + (part + 1) * ROWS, rows],
                matrix,
                FIRST,
                preferred_element_type=F32,
            )
            for part in range(2)
        )
        carried = reach * mm(local_ref[rows, width:], state)
        mixed_ref[rows, :] = (local_ref[rows, :width].astype(F32) + carried).astype(BF16)
    tile = 256
    for j in range(width_out // tile):
        columns = slice(j * tile, (j + 1) * tile)
        product = mm(mixed_ref[...], w_ref[:, columns]).astype(BF16)
        for d in range(pieces):
            out_ref[d, :, columns] = product[d * block : (d + 1) * block, :]


def regroup_kernel(target_ref, gain_ref, parts_ref, out_ref):
    owners, capacity, width = out_ref.shape
    pieces, rows, _ = parts_ref.shape
    projected = sum(parts_ref[k].astype(F32) for k in range(pieces))
    scale = lax.rsqrt(jnp.mean(projected * projected, axis=1, keepdims=True) + 1e-06)
    normed = (projected * scale * gain_ref[...]).astype(BF16)
    place = lax.broadcasted_iota(jnp.int32, (owners * capacity, rows), 0)
    select = (place == target_ref[...]).astype(BF16)
    out_ref[...] = mm(select, normed).astype(BF16).reshape(owners, capacity, width)


def call(kernel, outs, scratch, flops, moved, limit, *args, far=()):
    vmem = pl.BlockSpec(memory_space=pltpu.VMEM)
    hbm = pl.BlockSpec(memory_space=pltpu.HBM)
    return pl.pallas_call(
        kernel,
        out_shape=outs,
        in_specs=[hbm if k in far else vmem for k in range(len(args))],
        out_specs=jax.tree.map(lambda _: vmem, outs),
        scratch_shapes=scratch,
        cost_estimate=pl.CostEstimate(flops=flops, bytes_accessed=moved, transcendentals=0),
        compiler_params=pltpu.CompilerParams(vmem_limit_bytes=int(limit * 1024 * 1024)),
    )(*args)


def shards(head_inputs, b_proj, c_proj, log_decay, skip_gain, w_out, norm_gain, owner_ids):
    x, b, c, decays = head_inputs[0], b_proj[0], c_proj[0], log_decay.transpose(2, 0, 1)
    steps, width = x.shape
    heads = decays.shape[0]
    state_dim = b.shape[1]
    width_out = w_out.shape[1]
    times = lax.axis_size("tm")
    pieces = lax.axis_size("head")
    owners = times * lax.axis_size("farm")
    block = steps // pieces
    capacity = max(2, 2 * block // owners)
    depth = state_dim // times
    spec = jax.ShapeDtypeStruct
    wide = pltpu.VMEM((steps, width), BF16)
    narrow = pltpu.VMEM((steps, state_dim), BF16)
    state = pltpu.VMEM((state_dim, width), F32)
    parcel = call(
        state_kernel,
        spec((times, depth, width + LANES), BF16),
        [
            wide,
            narrow,
            pltpu.VMEM(decays.shape, F32),
            wide,
            state,
            pltpu.SemaphoreType.DMA((2 + steps // LANES,)),
        ],
        2 * steps * width * state_dim,
        2 * steps * width,
        63.4,
        x,
        b,
        decays,
        far=(0, 1, 2),
    )
    parcel = lax.all_to_all(parcel, "tm", split_axis=0, concat_axis=0, tiled=True)
    local = call(
        local_kernel,
        spec((steps + 2 * ROWS, width + state_dim), BF16),
        [
            wide,
            narrow,
            narrow,
            pltpu.VMEM(decays.shape, F32),
            state,
            pltpu.SemaphoreType.DMA((4,)),
        ],
        6 * steps * width * state_dim,
        8 * steps * width,
        61.5,
        x,
        b,
        c,
        decays,
        skip_gain[None, :],
        far=(0, 1, 2, 3),
    )
    parcel, local, w_late = lax.optimization_barrier((parcel, local, w_out))
    weights, local, target, gain, token = call(
        functools.partial(early_kernel, owners, capacity),
        (
            spec(w_out.shape, BF16),
            spec(local.shape, BF16),
            spec((1, block), jnp.int32),
            spec((1, width_out), F32),
            spec((ROWS, LANES), BF16),
        ),
        [pltpu.SemaphoreType.DMA((2,))],
        2 * owners * block * block,
        4 * width * width_out,
        48,
        w_late,
        local,
        owner_ids[0, :, 0][None, :],
        norm_gain[None, :],
        far=(0, 1),
    )
    prior = call(
        functools.partial(prefix_kernel, heads),
        spec((times, depth, width), BF16),
        [pltpu.VMEM((times * depth, width), F32)],
        2 * state_dim * width * LANES,
        4 * state_dim * width,
        16,
        parcel,
    )
    prior = lax.all_to_all(prior, "tm", split_axis=0, concat_axis=0, tiled=True)
    prior, token = lax.optimization_barrier((prior, token))
    token = lax.ppermute(token, "farm", [(0, 1), (1, 0)])
    prior, token = lax.optimization_barrier((prior, token))
    parts = call(
        functools.partial(project_kernel, heads),
        spec((pieces, block, width_out), BF16),
        [wide],
        2 * steps * width * (width_out + state_dim),
        2 * steps * (width + width_out) + 2 * width * width_out,
        24,
        local,
        prior,
        weights,
        token,
    )
    parts = lax.all_to_all(parts, "head", split_axis=0, concat_axis=0, tiled=True)
    outgoing = call(
        regroup_kernel,
        spec((owners, capacity, width_out), BF16),
        [],
        2 * owners * capacity * block * width_out,
        12 * block * width_out,
        16,
        target,
        gain,
        parts,
    )
    result = lax.all_to_all(outgoing, ("tm", "farm"), split_axis=0, concat_axis=0, tiled=True)
    return result[None, None]


def solution(mesh):
    placed = (
        P("farm", "tm", "head"),
        P("farm", "tm", None),
        P("farm", "tm", None),
        P("farm", "tm", "head"),
        P("head"),
        P("head", None),
        P(),
        P("farm", ("tm", "head"), None),
    )
    return jax.shard_map(
        shards,
        mesh=mesh,
        in_specs=placed,
        out_specs=P(("tm", "farm"), "head", None, None, None),
        check_vma=False,
    )
```

```python
import functools
import jax
import jax.numpy as jnp
from jax import lax
from jax.experimental import pallas as pl
from jax.experimental.pallas import tpu as pltpu
from jax.sharding import PartitionSpec as P

SPAN = 64
LANES = 128
ROWS = 16
SHELF = 64
TILE = 256
F32 = jnp.float32
BF16 = jnp.bfloat16
FIRST = (((0,), (0,)), ((), ()))
LAST = (((1,), (1,)), ((), ()))


def mm(a, b):
    return jnp.dot(a, b, preferred_element_type=F32)


def split2(value):
    high = value.astype(BF16)
    return high, (value - high.astype(F32)).astype(BF16)


def split3(value):
    high = value.astype(BF16)
    rest = value - high.astype(F32)
    middle = rest.astype(BF16)
    return high, middle, (rest - middle.astype(F32)).astype(BF16)


def head_spread(rows, width, group):
    head = lax.broadcasted_iota(jnp.int32, (rows, width), 0) * group
    lane = lax.broadcasted_iota(jnp.int32, (rows, width), 1)
    return ((lane >= head) & (lane < head + group)).astype(BF16)


def spread(value, matrix):
    high, low = split2(value)
    return lax.dot_general(high, matrix, FIRST, preferred_element_type=F32) + lax.dot_general(
        low, matrix, FIRST, preferred_element_type=F32
    )


def running(values, keep):
    length = values.shape[1]
    s = lax.broadcasted_iota(jnp.int32, (length, length), 0)
    t = lax.broadcasted_iota(jnp.int32, (length, length), 1)
    chosen = keep(s, t).astype(BF16)
    return sum(mm(part, chosen) for part in split3(values))


def fetch(pairs, sems):
    copies = [pltpu.make_async_copy(a, b, sems.at[i]) for i, (a, b) in enumerate(pairs)]
    for copy in copies:
        copy.start()
    return copies


def state_kernel(
    x_hbm, b_hbm, decay_hbm, out_ref, x_ref, b_ref, decay_ref, wx_ref, state_ref, sems
):
    heads, _, steps = decay_ref.shape
    width = x_ref.shape[1]
    blocks = [slice(k * LANES, (k + 1) * LANES) for k in range(steps // LANES)]
    first, second, *others = fetch(
        [(decay_hbm, decay_ref), (b_hbm, b_ref)]
        + [(x_hbm.at[rows, :], x_ref.at[rows, :]) for rows in blocks],
        sems,
    )
    matrix = head_spread(heads, width, width // heads)
    later = jnp.zeros((heads, 1), F32)
    weights = [None] * len(blocks)
    first.wait()
    for k in reversed(range(len(blocks))):
        values = decay_ref[:, 0, blocks[k]]
        weights[k] = jnp.exp(running(values, lambda s, t: s > t) + later)
        later = later + jnp.sum(values, axis=1, keepdims=True)
    second.wait()
    across = b_ref[...].T
    for rows, weight, copy in zip(blocks, weights, others):
        weight = spread(weight, matrix)
        copy.wait()
        wx_ref[rows, :] = (x_ref[rows, :].astype(F32) * weight).astype(BF16)
    state_ref[...] = mm(across, wx_ref[...])
    parcels, depth, _ = out_ref.shape
    unit = head_spread(heads, LANES, 1)
    tail = [
        lax.dot_general(part, unit, FIRST, preferred_element_type=F32)[0:1]
        for part in split2(jnp.broadcast_to(later, (heads, LANES)))
    ]
    out_ref[:, :, :width] = state_ref[...].astype(BF16).reshape(parcels, depth, width)
    tail = jnp.concatenate(tail, axis=0).astype(BF16)
    for k in range(parcels):
        out_ref[k, :, width:] = tail


def prefix_kernel(heads, in_ref, out_ref, factor_ref):
    parcels, depth, width = out_ref.shape
    matrix = head_spread(LANES, width, width // heads)
    pairs = head_spread(parcels, parcels * depth, depth)
    logs = mm(pairs, in_ref[:, :, width:].reshape(parcels * depth, LANES))
    factor_ref[...] = sum(mm(part, matrix) for part in split2(jnp.exp(logs)))
    carried = jnp.zeros((depth, width), F32)
    for k in range(parcels):
        out_ref[k] = carried.astype(BF16)
        carried = factor_ref[k : k + 1, :] * carried + in_ref[k, :, :width].astype(F32)


def local_kernel(
    x_hbm,
    b_hbm,
    c_hbm,
    decay_hbm,
    skip_ref,
    out_ref,
    x_ref,
    b_ref,
    c_ref,
    decay_ref,
    state_ref,
    sems,
):
    copies = fetch(
        ((decay_hbm, decay_ref), (x_hbm, x_ref), (b_hbm, b_ref), (c_hbm, c_ref)), sems
    )
    heads, _, steps = decay_ref.shape
    width = x_ref.shape[1]
    matrix = head_spread(heads, width, width // heads)
    row = lax.broadcasted_iota(jnp.int32, (SPAN, SPAN), 0)
    column = lax.broadcasted_iota(jnp.int32, (SPAN, SPAN), 1)
    causal = row >= column
    first = lax.broadcasted_iota(jnp.int32, (heads, LANES), 1) < SPAN
    skip = sum(mm(part, matrix) for part in split3(skip_ref[...]))
    for copy in copies:
        copy.wait()
    before = jnp.zeros((heads, 1), F32)
    for k in range(steps // LANES):
        lanes = slice(k * LANES, (k + 1) * LANES)
        values = decay_ref[:, 0, lanes]
        reach = jnp.exp(running(values, lambda s, t: s <= t) + before)
        reach = jnp.concatenate([reach, jnp.zeros((ROWS - heads, LANES), F32)], axis=0)
        for part, half in enumerate(split2(reach)):
            out_ref[steps + part * ROWS : steps + (part + 1) * ROWS, lanes] = half
        before = before + jnp.sum(values, axis=1, keepdims=True)
        local = running(values, lambda s, t: (s <= t) & ((s < SPAN) == (t < SPAN)))
        middle = 0.5 * jnp.where(
            first, local[:, SPAN - 1 : SPAN], local[:, LANES - 1 : LANES]
        )
        ups = spread(jnp.exp(local - middle), matrix)
        downs = spread(jnp.exp(middle - local), matrix)
        for part in range(LANES // SPAN):
            inner = slice(part * SPAN, (part + 1) * SPAN)
            rows = slice(k * LANES + part * SPAN, k * LANES + (part + 1) * SPAN)
            up = ups[inner]
            half = up[SPAN - 1 : SPAN, :]
            x = x_ref[rows, :].astype(F32)
            b = b_ref[rows, :]
            c = c_ref[rows, :]
            scaled = (x * downs[inner]).astype(BF16)
            scores = lax.dot_general(c, b, LAST, preferred_element_type=F32)
            scores = jnp.where(causal, scores, 0.0).astype(BF16)
            y = mm(scores, scaled)
            update = lax.dot_general(b, scaled, FIRST, preferred_element_type=F32)
            if rows.start == 0:
                state_ref[...] = half * update
            else:
                state = state_ref[...]
                y = y + mm(c, (state * half).astype(BF16))
                state_ref[...] = half * (half * state + update)
            out_ref[rows, :width] = (up * y + skip * x).astype(BF16)
            out_ref[rows, width:] = c


def early_kernel(local_hbm, w_hbm, local_ref, shelf_hbm, sems):
    copies = fetch(
        [(local_hbm, local_ref)]
        + [
            (w_hbm.at[:, k * TILE : (k + 1) * TILE], shelf_hbm.at[k])
            for k in range(w_hbm.shape[1] // TILE)
        ],
        sems,
    )
    for copy in copies:
        copy.wait()


def project_kernel(heads, index_ref, local_ref, prior_ref, w_hbm, *rest):
    outs, (mixed_ref, w_ref, sems) = rest[:-3], rest[-3:]
    copies = fetch([(w_hbm.at[k], w_ref.at[k]) for k in range(w_ref.shape[0])], sems)
    steps = mixed_ref.shape[0]
    parcels, depth, width = prior_ref.shape
    pieces = len(outs)
    block, width_out = outs[0].shape
    state = prior_ref[...].reshape(parcels * depth, width)
    matrix = head_spread(ROWS, width, width // heads)
    for k in range(pieces):
        rows = slice(k * block, (k + 1) * block)
        reach = sum(
            lax.dot_general(
                local_ref[steps + part * ROWS : steps + (part + 1) * ROWS, rows],
                matrix,
                FIRST,
                preferred_element_type=F32,
            )
            for part in range(2)
        )
        carried = reach * mm(local_ref[rows, width:], state)
        ahead = lax.rem(k - index_ref[0] + pieces, pieces)
        mixed_ref[pl.ds(pl.multiple_of(ahead * block, block), block), :] = (
            local_ref[rows, :width].astype(F32) + carried
        ).astype(BF16)
    for k, copy in enumerate(copies):
        columns = slice(k * TILE, (k + 1) * TILE)
        copy.wait()
        product = mm(mixed_ref[...], w_ref[k]).astype(BF16)
        for d in range(pieces):
            outs[d][:, columns] = product[d * block : (d + 1) * block, :]


def regroup_kernel(routes_ref, gain_ref, *rest):
    parts, out_ref = rest[:-1], rest[-1]
    owners, capacity, width = out_ref.shape
    rows = parts[0].shape[0]
    routes = routes_ref[...]
    named = lax.broadcasted_iota(jnp.int32, (owners, rows), 0) == routes
    before = lax.broadcasted_iota(jnp.int32, (rows, rows), 0) < lax.broadcasted_iota(
        jnp.int32, (rows, rows), 1
    )
    earlier = mm(named.astype(BF16), before.astype(BF16))
    slot = jnp.sum(jnp.where(named, earlier, 0.0), axis=0, keepdims=True)
    target = routes * capacity + slot.astype(jnp.int32)
    projected = sum(part[...].astype(F32) for part in parts)
    scale = lax.rsqrt(jnp.mean(projected * projected, axis=1, keepdims=True) + 1e-06)
    normed = (projected * scale * gain_ref[...]).astype(BF16)
    place = lax.broadcasted_iota(jnp.int32, (owners * capacity, rows), 0)
    select = (place == target).astype(BF16)
    out_ref[...] = mm(select, normed).astype(BF16).reshape(owners, capacity, width)


def call(kernel, outs, scratch, flops, moved, limit, *args, far=(), far_out=(), scalars=()):
    vmem = pl.BlockSpec(memory_space=pltpu.VMEM)
    hbm = pl.BlockSpec(memory_space=pltpu.HBM)
    smem = pl.BlockSpec(memory_space=pltpu.SMEM)
    return pl.pallas_call(
        kernel,
        out_shape=outs,
        in_specs=[hbm if k in far else smem if k in scalars else vmem for k in range(len(args))],
        out_specs=tuple(hbm if k in far_out else vmem for k in range(len(outs)))
        if isinstance(outs, tuple)
        else vmem,
        scratch_shapes=scratch,
        cost_estimate=pl.CostEstimate(flops=flops, bytes_accessed=moved, transcendentals=0),
        compiler_params=pltpu.CompilerParams(vmem_limit_bytes=int(limit * 1024 * 1024)),
    )(*args)


def shards(head_inputs, b_proj, c_proj, log_decay, skip_gain, w_out, norm_gain, owner_ids):
    x, b, c, decays = head_inputs[0], b_proj[0], c_proj[0], log_decay.transpose(2, 0, 1)
    steps, width = x.shape
    heads = decays.shape[0]
    state_dim = b.shape[1]
    width_out = w_out.shape[1]
    times = lax.axis_size("tm")
    pieces = lax.axis_size("head")
    owners = times * lax.axis_size("farm")
    block = steps // pieces
    capacity = max(2, 2 * block // owners)
    depth = state_dim // times
    spec = jax.ShapeDtypeStruct
    wide = pltpu.VMEM((steps, width), BF16)
    narrow = pltpu.VMEM((steps, state_dim), BF16)
    state = pltpu.VMEM((state_dim, width), F32)
    parcel = call(
        state_kernel,
        spec((times, depth, width + LANES), BF16),
        [
            wide,
            narrow,
            pltpu.VMEM(decays.shape, F32),
            wide,
            state,
            pltpu.SemaphoreType.DMA((2 + steps // LANES,)),
        ],
        2 * steps * width * state_dim,
        2 * steps * width,
        63.4,
        x,
        b,
        decays,
        far=(0, 1, 2),
    )
    parcel = lax.all_to_all(parcel, "tm", split_axis=0, concat_axis=0, tiled=True)
    local = call(
        local_kernel,
        spec((steps + 2 * ROWS, width + state_dim), BF16),
        [
            wide,
            narrow,
            narrow,
            pltpu.VMEM(decays.shape, F32),
            state,
            pltpu.SemaphoreType.DMA((4,)),
        ],
        6 * steps * width * state_dim,
        8 * steps * width,
        61.5,
        x,
        b,
        c,
        decays,
        skip_gain[None, :],
        far=(0, 1, 2, 3),
    )
    parcel, local, w_late = lax.optimization_barrier((parcel, local, w_out))
    local, shelf = call(
        early_kernel,
        (spec(local.shape, BF16), spec((SHELF, width, TILE), BF16)),
        [pltpu.SemaphoreType.DMA((1 + width_out // TILE,))],
        0,
        4 * width * width_out,
        48,
        local,
        w_late,
        far=(0, 1),
        far_out=(1,),
    )
    prior = call(
        functools.partial(prefix_kernel, heads),
        spec((times, depth, width), BF16),
        [pltpu.VMEM((times, width), F32)],
        2 * state_dim * width * LANES,
        4 * state_dim * width,
        16,
        parcel,
    )
    prior = lax.all_to_all(prior, "tm", split_axis=0, concat_axis=0, tiled=True)
    index = lax.axis_index("head").astype(jnp.int32).reshape(1)
    parts = call(
        functools.partial(project_kernel, heads),
        (spec((block, width_out), BF16),) * pieces,
        [
            wide,
            pltpu.VMEM((width_out // TILE, width, TILE), BF16),
            pltpu.SemaphoreType.DMA((width_out // TILE,)),
        ],
        2 * steps * width * (width_out + state_dim),
        2 * steps * (width + width_out) + 2 * width * width_out,
        40,
        index,
        local,
        prior,
        shelf,
        far=(3,),
        scalars=(0,),
    )
    ring = range(pieces)
    moved = [
        lax.ppermute(parts[d], "head", [(k, (k + d) % pieces) for k in ring]) for d in (2, 1, 3)
    ]
    outgoing = call(
        regroup_kernel,
        spec((owners, capacity, width_out), BF16),
        [],
        2 * owners * capacity * block * width_out,
        12 * block * width_out,
        16,
        owner_ids[0, :, 0][None, :],
        norm_gain[None, :],
        parts[0],
        *moved,
    )
    result = lax.all_to_all(outgoing, ("tm", "farm"), split_axis=0, concat_axis=0, tiled=True)
    return result[None, None]


def solution(mesh):
    placed = (
        P("farm", "tm", "head"),
        P("farm", "tm", None),
        P("farm", "tm", None),
        P("farm", "tm", "head"),
        P("head"),
        P("head", None),
        P(),
        P("farm", ("tm", "head"), None),
    )
    return jax.shard_map(
        shards,
        mesh=mesh,
        in_specs=placed,
        out_specs=P(("tm", "farm"), "head", None, None, None),
        check_vma=False,
    )
```

```python
import functools
import jax
import jax.numpy as jnp
from jax import lax
from jax.experimental import pallas as pl
from jax.experimental.pallas import tpu as pltpu
from jax.sharding import PartitionSpec as P

SPAN = 64
LANES = 128
ROWS = 16
TILE = 256
F32 = jnp.float32
BF16 = jnp.bfloat16
FIRST = (((0,), (0,)), ((), ()))
LAST = (((1,), (1,)), ((), ()))


def mm(a, b):
    return jnp.dot(a, b, preferred_element_type=F32)


def split2(value):
    high = value.astype(BF16)
    return high, (value - high.astype(F32)).astype(BF16)


def split3(value):
    high = value.astype(BF16)
    rest = value - high.astype(F32)
    middle = rest.astype(BF16)
    return high, middle, (rest - middle.astype(F32)).astype(BF16)


def head_spread(rows, width, group):
    head = lax.broadcasted_iota(jnp.int32, (rows, width), 0) * group
    lane = lax.broadcasted_iota(jnp.int32, (rows, width), 1)
    return ((lane >= head) & (lane < head + group)).astype(BF16)


def spread(value, matrix):
    high, low = split2(value)
    return lax.dot_general(high, matrix, FIRST, preferred_element_type=F32) + lax.dot_general(
        low, matrix, FIRST, preferred_element_type=F32
    )


def running(values, keep):
    length = values.shape[1]
    s = lax.broadcasted_iota(jnp.int32, (length, length), 0)
    t = lax.broadcasted_iota(jnp.int32, (length, length), 1)
    chosen = keep(s, t).astype(BF16)
    return sum(mm(part, chosen) for part in split3(values))


def fetch(pairs, sems):
    copies = [pltpu.make_async_copy(a, b, sems.at[i]) for i, (a, b) in enumerate(pairs)]
    for copy in copies:
        copy.start()
    return copies


def state_kernel(
    x_hbm, b_hbm, decay_hbm, out_ref, x_ref, b_ref, decay_ref, wx_ref, state_ref, sems
):
    heads, _, steps = decay_ref.shape
    width = x_ref.shape[1]
    blocks = [slice(k * LANES, (k + 1) * LANES) for k in range(steps // LANES)]
    first, second, *others = fetch(
        [(decay_hbm, decay_ref), (b_hbm, b_ref)]
        + [(x_hbm.at[rows, :], x_ref.at[rows, :]) for rows in blocks],
        sems,
    )
    matrix = head_spread(heads, width, width // heads)
    later = jnp.zeros((heads, 1), F32)
    weights = [None] * len(blocks)
    first.wait()
    for k in reversed(range(len(blocks))):
        values = decay_ref[:, 0, blocks[k]]
        weights[k] = jnp.exp(running(values, lambda s, t: s > t) + later)
        later = later + jnp.sum(values, axis=1, keepdims=True)
    second.wait()
    across = b_ref[...].T
    for rows, weight, copy in zip(blocks, weights, others):
        weight = spread(weight, matrix)
        copy.wait()
        wx_ref[rows, :] = (x_ref[rows, :].astype(F32) * weight).astype(BF16)
    state_ref[...] = mm(across, wx_ref[...])
    parcels, depth, _ = out_ref.shape
    unit = head_spread(heads, LANES, 1)
    tail = [
        lax.dot_general(part, unit, FIRST, preferred_element_type=F32)[0:1]
        for part in split2(jnp.broadcast_to(later, (heads, LANES)))
    ]
    out_ref[:, :, :width] = state_ref[...].astype(BF16).reshape(parcels, depth, width)
    tail = jnp.concatenate(tail, axis=0).astype(BF16)
    for k in range(parcels):
        out_ref[k, :, width:] = tail


def prefix_kernel(heads, in_ref, out_ref, factor_ref):
    parcels, depth, width = out_ref.shape
    matrix = head_spread(LANES, width, width // heads)
    pairs = head_spread(parcels, parcels * depth, depth)
    logs = mm(pairs, in_ref[:, :, width:].reshape(parcels * depth, LANES))
    factor_ref[...] = sum(mm(part, matrix) for part in split2(jnp.exp(logs)))
    carried = jnp.zeros((depth, width), F32)
    for k in range(parcels):
        out_ref[k] = carried.astype(BF16)
        carried = factor_ref[k : k + 1, :] * carried + in_ref[k, :, :width].astype(F32)


def local_kernel(
    x_hbm,
    b_hbm,
    c_hbm,
    decay_hbm,
    skip_ref,
    out_ref,
    x_ref,
    b_ref,
    c_ref,
    decay_ref,
    state_ref,
    sems,
):
    copies = fetch(
        ((decay_hbm, decay_ref), (x_hbm, x_ref), (b_hbm, b_ref), (c_hbm, c_ref)), sems
    )
    heads, _, steps = decay_ref.shape
    width = x_ref.shape[1]
    matrix = head_spread(heads, width, width // heads)
    row = lax.broadcasted_iota(jnp.int32, (SPAN, SPAN), 0)
    column = lax.broadcasted_iota(jnp.int32, (SPAN, SPAN), 1)
    causal = row >= column
    first = lax.broadcasted_iota(jnp.int32, (heads, LANES), 1) < SPAN
    skip = sum(mm(part, matrix) for part in split3(skip_ref[...]))
    for copy in copies:
        copy.wait()
    before = jnp.zeros((heads, 1), F32)
    for k in range(steps // LANES):
        lanes = slice(k * LANES, (k + 1) * LANES)
        values = decay_ref[:, 0, lanes]
        reach = jnp.exp(running(values, lambda s, t: s <= t) + before)
        reach = jnp.concatenate([reach, jnp.zeros((ROWS - heads, LANES), F32)], axis=0)
        for part, half in enumerate(split2(reach)):
            out_ref[steps + part * ROWS : steps + (part + 1) * ROWS, lanes] = half
        before = before + jnp.sum(values, axis=1, keepdims=True)
        local = running(values, lambda s, t: (s <= t) & ((s < SPAN) == (t < SPAN)))
        middle = 0.5 * jnp.where(
            first, local[:, SPAN - 1 : SPAN], local[:, LANES - 1 : LANES]
        )
        ups = spread(jnp.exp(local - middle), matrix)
        downs = spread(jnp.exp(middle - local), matrix)
        for part in range(LANES // SPAN):
            inner = slice(part * SPAN, (part + 1) * SPAN)
            rows = slice(k * LANES + part * SPAN, k * LANES + (part + 1) * SPAN)
            up = ups[inner]
            half = up[SPAN - 1 : SPAN, :]
            x = x_ref[rows, :].astype(F32)
            b = b_ref[rows, :]
            c = c_ref[rows, :]
            scaled = (x * downs[inner]).astype(BF16)
            scores = lax.dot_general(c, b, LAST, preferred_element_type=F32)
            scores = jnp.where(causal, scores, 0.0).astype(BF16)
            y = mm(scores, scaled)
            update = lax.dot_general(b, scaled, FIRST, preferred_element_type=F32)
            if rows.start == 0:
                state_ref[...] = half * update
            else:
                state = state_ref[...]
                y = y + mm(c, (state * half).astype(BF16))
                state_ref[...] = half * (half * state + update)
            out_ref[rows, :width] = (up * y + skip * x).astype(BF16)
            out_ref[rows, width:] = c


def early_kernel(local_hbm, local_ref, sems):
    (copy,) = fetch(((local_hbm, local_ref),), sems)
    copy.wait()


def project_kernel(heads, index_ref, local_ref, prior_ref, w_ref, *rest):
    outs, mixed_ref = rest[:-1], rest[-1]
    tiles = [slice(k, k + TILE) for k in range(0, w_ref.shape[1], TILE)]
    steps = mixed_ref.shape[0]
    parcels, depth, width = prior_ref.shape
    pieces = len(outs)
    block, width_out = outs[0].shape
    state = prior_ref[...].reshape(parcels * depth, width)
    matrix = head_spread(ROWS, width, width // heads)
    for k in range(pieces):
        rows = slice(k * block, (k + 1) * block)
        reach = sum(
            lax.dot_general(
                local_ref[steps + part * ROWS : steps + (part + 1) * ROWS, rows],
                matrix,
                FIRST,
                preferred_element_type=F32,
            )
            for part in range(2)
        )
        carried = reach * mm(local_ref[rows, width:], state)
        ahead = lax.rem(k - index_ref[0] + pieces, pieces)
        mixed_ref[pl.ds(pl.multiple_of(ahead * block, block), block), :] = (
            local_ref[rows, :width].astype(F32) + carried
        ).astype(BF16)
    for columns in tiles:
        product = mm(mixed_ref[...], w_ref[:, columns]).astype(BF16)
        for d in range(pieces):
            outs[d][:, columns] = product[d * block : (d + 1) * block, :]


def regroup_kernel(routes_ref, gain_ref, *rest):
    parts, out_ref = rest[:-1], rest[-1]
    owners, capacity, width = out_ref.shape
    rows = parts[0].shape[0]
    routes = routes_ref[...]
    named = lax.broadcasted_iota(jnp.int32, (owners, rows), 0) == routes
    before = lax.broadcasted_iota(jnp.int32, (rows, rows), 0) < lax.broadcasted_iota(
        jnp.int32, (rows, rows), 1
    )
    earlier = mm(named.astype(BF16), before.astype(BF16))
    slot = jnp.sum(jnp.where(named, earlier, 0.0), axis=0, keepdims=True)
    target = routes * capacity + slot.astype(jnp.int32)
    projected = sum(part[...].astype(F32) for part in parts)
    scale = lax.rsqrt(jnp.mean(projected * projected, axis=1, keepdims=True) + 1e-06)
    normed = (projected * scale * gain_ref[...]).astype(BF16)
    place = lax.broadcasted_iota(jnp.int32, (owners * capacity, rows), 0)
    select = (place == target).astype(BF16)
    out_ref[...] = mm(select, normed).astype(BF16).reshape(owners, capacity, width)


def call(kernel, outs, scratch, flops, moved, limit, *args, far=(), scalars=()):
    vmem = pl.BlockSpec(memory_space=pltpu.VMEM)
    hbm = pl.BlockSpec(memory_space=pltpu.HBM)
    smem = pl.BlockSpec(memory_space=pltpu.SMEM)
    return pl.pallas_call(
        kernel,
        out_shape=outs,
        in_specs=[hbm if k in far else smem if k in scalars else vmem for k in range(len(args))],
        out_specs=jax.tree.map(lambda _: vmem, outs),
        scratch_shapes=scratch,
        cost_estimate=pl.CostEstimate(flops=flops, bytes_accessed=moved, transcendentals=0),
        compiler_params=pltpu.CompilerParams(vmem_limit_bytes=int(limit * 1024 * 1024)),
    )(*args)


def shards(head_inputs, b_proj, c_proj, log_decay, skip_gain, w_out, norm_gain, owner_ids):
    x, b, c, decays = head_inputs[0], b_proj[0], c_proj[0], log_decay.transpose(2, 0, 1)
    steps, width = x.shape
    heads = decays.shape[0]
    state_dim = b.shape[1]
    width_out = w_out.shape[1]
    times = lax.axis_size("tm")
    pieces = lax.axis_size("head")
    owners = times * lax.axis_size("farm")
    block = steps // pieces
    capacity = max(2, 2 * block // owners)
    depth = state_dim // times
    spec = jax.ShapeDtypeStruct
    wide = pltpu.VMEM((steps, width), BF16)
    narrow = pltpu.VMEM((steps, state_dim), BF16)
    state = pltpu.VMEM((state_dim, width), F32)
    parcel = call(
        state_kernel,
        spec((times, depth, width + LANES), BF16),
        [
            wide,
            narrow,
            pltpu.VMEM(decays.shape, F32),
            wide,
            state,
            pltpu.SemaphoreType.DMA((2 + steps // LANES,)),
        ],
        2 * steps * width * state_dim,
        2 * steps * width,
        63.4,
        x,
        b,
        decays,
        far=(0, 1, 2),
    )
    parcel = lax.all_to_all(parcel, "tm", split_axis=0, concat_axis=0, tiled=True)
    local = call(
        local_kernel,
        spec((steps + 2 * ROWS, width + state_dim), BF16),
        [
            wide,
            narrow,
            narrow,
            pltpu.VMEM(decays.shape, F32),
            state,
            pltpu.SemaphoreType.DMA((4,)),
        ],
        6 * steps * width * state_dim,
        8 * steps * width,
        61.5,
        x,
        b,
        c,
        decays,
        skip_gain[None, :],
        far=(0, 1, 2, 3),
    )
    parcel, local = lax.optimization_barrier((parcel, local))
    local = call(
        early_kernel,
        spec(local.shape, BF16),
        [pltpu.SemaphoreType.DMA((1,))],
        0,
        4 * steps * width,
        16,
        local,
        far=(0,),
    )
    prior = call(
        functools.partial(prefix_kernel, heads),
        spec((times, depth, width), BF16),
        [pltpu.VMEM((times, width), F32)],
        2 * state_dim * width * LANES,
        4 * state_dim * width,
        16,
        parcel,
    )
    prior = lax.all_to_all(prior, "tm", split_axis=0, concat_axis=0, tiled=True)
    index = lax.axis_index("head").astype(jnp.int32).reshape(1)
    parts = call(
        functools.partial(project_kernel, heads),
        (spec((block, width_out), BF16),) * pieces,
        [wide],
        2 * steps * width * (width_out + state_dim),
        2 * steps * (width + width_out) + 2 * width * width_out,
        24,
        index,
        local,
        prior,
        w_out,
        scalars=(0,),
    )
    ring = range(pieces)
    moved = [
        lax.ppermute(parts[d], "head", [(k, (k + d) % pieces) for k in ring]) for d in (2, 1, 3)
    ]
    outgoing = call(
        regroup_kernel,
        spec((owners, capacity, width_out), BF16),
        [],
        2 * owners * capacity * block * width_out,
        12 * block * width_out,
        16,
        owner_ids[0, :, 0][None, :],
        norm_gain[None, :],
        parts[0],
        *moved,
    )
    result = lax.all_to_all(outgoing, ("tm", "farm"), split_axis=0, concat_axis=0, tiled=True)
    return result[None, None]


def solution(mesh):
    placed = (
        P("farm", "tm", "head"),
        P("farm", "tm", None),
        P("farm", "tm", None),
        P("farm", "tm", "head"),
        P("head"),
        P("head", None),
        P(),
        P("farm", ("tm", "head"), None),
    )
    return jax.shard_map(
        shards,
        mesh=mesh,
        in_specs=placed,
        out_specs=P(("tm", "farm"), "head", None, None, None),
        check_vma=False,
    )
```

```python
import functools
import jax
import jax.numpy as jnp
from jax import lax
from jax.experimental import pallas as pl
from jax.experimental.pallas import tpu as pltpu
from jax.sharding import PartitionSpec as P

SPAN = 64
LANES = 128
ROWS = 16
F32 = jnp.float32
BF16 = jnp.bfloat16
FIRST = (((0,), (0,)), ((), ()))
LAST = (((1,), (1,)), ((), ()))


def mm(a, b):
    return jnp.dot(a, b, preferred_element_type=F32)


def split2(value):
    high = value.astype(BF16)
    return high, (value - high.astype(F32)).astype(BF16)


def split3(value):
    high = value.astype(BF16)
    rest = value - high.astype(F32)
    middle = rest.astype(BF16)
    return high, middle, (rest - middle.astype(F32)).astype(BF16)


def head_spread(rows, width, group):
    head = lax.broadcasted_iota(jnp.int32, (rows, width), 0) * group
    lane = lax.broadcasted_iota(jnp.int32, (rows, width), 1)
    return ((lane >= head) & (lane < head + group)).astype(BF16)


def spread(value, matrix):
    high, low = split2(value)
    return lax.dot_general(high, matrix, FIRST, preferred_element_type=F32) + lax.dot_general(
        low, matrix, FIRST, preferred_element_type=F32
    )


def running(values, keep):
    length = values.shape[1]
    s = lax.broadcasted_iota(jnp.int32, (length, length), 0)
    t = lax.broadcasted_iota(jnp.int32, (length, length), 1)
    chosen = keep(s, t).astype(BF16)
    return sum(mm(part, chosen) for part in split3(values))


def fetch(pairs, sems):
    copies = [pltpu.make_async_copy(a, b, sems.at[i]) for i, (a, b) in enumerate(pairs)]
    for copy in copies:
        copy.start()
    return copies


def state_kernel(
    x_hbm, b_hbm, decay_hbm, out_ref, x_ref, b_ref, decay_ref, wx_ref, state_ref, sems
):
    heads, _, steps = decay_ref.shape
    width = x_ref.shape[1]
    blocks = [slice(k * LANES, (k + 1) * LANES) for k in range(steps // LANES)]
    first, second, *others = fetch(
        [(decay_hbm, decay_ref), (b_hbm, b_ref)]
        + [(x_hbm.at[rows, :], x_ref.at[rows, :]) for rows in blocks],
        sems,
    )
    matrix = head_spread(heads, width, width // heads)
    later = jnp.zeros((heads, 1), F32)
    weights = [None] * len(blocks)
    first.wait()
    for k in reversed(range(len(blocks))):
        values = decay_ref[:, 0, blocks[k]]
        weights[k] = jnp.exp(running(values, lambda s, t: s > t) + later)
        later = later + jnp.sum(values, axis=1, keepdims=True)
    second.wait()
    across = b_ref[...].T
    for rows, weight, copy in zip(blocks, weights, others):
        weight = spread(weight, matrix)
        copy.wait()
        wx_ref[rows, :] = (x_ref[rows, :].astype(F32) * weight).astype(BF16)
    state_ref[...] = mm(across, wx_ref[...])
    parcels, depth, _ = out_ref.shape
    unit = head_spread(heads, LANES, 1)
    tail = [
        lax.dot_general(part, unit, FIRST, preferred_element_type=F32)[0:1]
        for part in split2(jnp.broadcast_to(later, (heads, LANES)))
    ]
    out_ref[:, :, :width] = state_ref[...].astype(BF16).reshape(parcels, depth, width)
    tail = jnp.concatenate(tail, axis=0).astype(BF16)
    for k in range(parcels):
        out_ref[k, :, width:] = tail


def prefix_kernel(heads, in_ref, out_ref, factor_ref):
    parcels, depth, width = out_ref.shape
    matrix = head_spread(LANES, width, width // heads)
    pairs = head_spread(parcels, parcels * depth, depth)
    logs = mm(pairs, in_ref[:, :, width:].reshape(parcels * depth, LANES))
    factor_ref[...] = sum(mm(part, matrix) for part in split2(jnp.exp(logs)))
    carried = jnp.zeros((depth, width), F32)
    for k in range(parcels):
        out_ref[k] = carried.astype(BF16)
        carried = factor_ref[k : k + 1, :] * carried + in_ref[k, :, :width].astype(F32)


def local_kernel(
    x_hbm,
    b_hbm,
    c_hbm,
    decay_hbm,
    skip_ref,
    out_ref,
    x_ref,
    b_ref,
    c_ref,
    decay_ref,
    state_ref,
    sems,
):
    copies = fetch(
        ((decay_hbm, decay_ref), (x_hbm, x_ref), (b_hbm, b_ref), (c_hbm, c_ref)), sems
    )
    heads, _, steps = decay_ref.shape
    width = x_ref.shape[1]
    matrix = head_spread(heads, width, width // heads)
    row = lax.broadcasted_iota(jnp.int32, (SPAN, SPAN), 0)
    column = lax.broadcasted_iota(jnp.int32, (SPAN, SPAN), 1)
    causal = row >= column
    first = lax.broadcasted_iota(jnp.int32, (heads, LANES), 1) < SPAN
    skip = sum(mm(part, matrix) for part in split3(skip_ref[...]))
    for copy in copies:
        copy.wait()
    before = jnp.zeros((heads, 1), F32)
    for k in range(steps // LANES):
        lanes = slice(k * LANES, (k + 1) * LANES)
        values = decay_ref[:, 0, lanes]
        reach = jnp.exp(running(values, lambda s, t: s <= t) + before)
        reach = jnp.concatenate([reach, jnp.zeros((ROWS - heads, LANES), F32)], axis=0)
        for part, half in enumerate(split2(reach)):
            out_ref[steps + part * ROWS : steps + (part + 1) * ROWS, lanes] = half
        before = before + jnp.sum(values, axis=1, keepdims=True)
        local = running(values, lambda s, t: (s <= t) & ((s < SPAN) == (t < SPAN)))
        middle = 0.5 * jnp.where(
            first, local[:, SPAN - 1 : SPAN], local[:, LANES - 1 : LANES]
        )
        ups = spread(jnp.exp(local - middle), matrix)
        downs = spread(jnp.exp(middle - local), matrix)
        for part in range(LANES // SPAN):
            inner = slice(part * SPAN, (part + 1) * SPAN)
            rows = slice(k * LANES + part * SPAN, k * LANES + (part + 1) * SPAN)
            up = ups[inner]
            half = up[SPAN - 1 : SPAN, :]
            x = x_ref[rows, :].astype(F32)
            b = b_ref[rows, :]
            c = c_ref[rows, :]
            scaled = (x * downs[inner]).astype(BF16)
            scores = lax.dot_general(c, b, LAST, preferred_element_type=F32)
            scores = jnp.where(causal, scores, 0.0).astype(BF16)
            y = mm(scores, scaled)
            update = lax.dot_general(b, scaled, FIRST, preferred_element_type=F32)
            if rows.start == 0:
                state_ref[...] = half * update
            else:
                state = state_ref[...]
                y = y + mm(c, (state * half).astype(BF16))
                state_ref[...] = half * (half * state + update)
            out_ref[rows, :width] = (up * y + skip * x).astype(BF16)
            out_ref[rows, width:] = c


def early_kernel(
    owners,
    capacity,
    w_hbm,
    local_hbm,
    routes_ref,
    gain_ref,
    w_ref,
    local_ref,
    target_ref,
    gain_out_ref,
    sems,
):
    copies = fetch(((w_hbm, w_ref), (local_hbm, local_ref)), sems)
    routes = routes_ref[...]
    rows = routes.shape[1]
    named = lax.broadcasted_iota(jnp.int32, (owners, rows), 0) == routes
    before = lax.broadcasted_iota(jnp.int32, (rows, rows), 0) < lax.broadcasted_iota(
        jnp.int32, (rows, rows), 1
    )
    earlier = mm(named.astype(BF16), before.astype(BF16))
    slot = jnp.sum(jnp.where(named, earlier, 0.0), axis=0, keepdims=True)
    target_ref[...] = routes * capacity + slot.astype(jnp.int32)
    gain_out_ref[...] = gain_ref[...]
    for copy in copies:
        copy.wait()


def project_kernel(heads, local_ref, prior_ref, w_ref, out_ref, mixed_ref):
    steps = mixed_ref.shape[0]
    parcels, depth, width = prior_ref.shape
    pieces, block, width_out = out_ref.shape
    state = prior_ref[...].reshape(parcels * depth, width)
    matrix = head_spread(ROWS, width, width // heads)
    for k in range(steps // LANES):
        rows = slice(k * LANES, (k + 1) * LANES)
        reach = sum(
            lax.dot_general(
                local_ref[steps + part * ROWS : steps + (part + 1) * ROWS, rows],
                matrix,
                FIRST,
                preferred_element_type=F32,
            )
            for part in range(2)
        )
        carried = reach * mm(local_ref[rows, width:], state)
        mixed_ref[rows, :] = (local_ref[rows, :width].astype(F32) + carried).astype(BF16)
    tile = 256
    for j in range(width_out // tile):
        columns = slice(j * tile, (j + 1) * tile)
        product = mm(mixed_ref[...], w_ref[:, columns]).astype(BF16)
        for d in range(pieces):
            out_ref[d, :, columns] = product[d * block : (d + 1) * block, :]


def regroup_kernel(target_ref, gain_ref, parts_ref, out_ref):
    owners, capacity, width = out_ref.shape
    pieces, rows, _ = parts_ref.shape
    projected = sum(parts_ref[k].astype(F32) for k in range(pieces))
    scale = lax.rsqrt(jnp.mean(projected * projected, axis=1, keepdims=True) + 1e-06)
    normed = (projected * scale * gain_ref[...]).astype(BF16)
    place = lax.broadcasted_iota(jnp.int32, (owners * capacity, rows), 0)
    select = (place == target_ref[...]).astype(BF16)
    out_ref[...] = mm(select, normed).astype(BF16).reshape(owners, capacity, width)


def call(kernel, outs, scratch, flops, moved, limit, *args, far=()):
    vmem = pl.BlockSpec(memory_space=pltpu.VMEM)
    hbm = pl.BlockSpec(memory_space=pltpu.HBM)
    return pl.pallas_call(
        kernel,
        out_shape=outs,
        in_specs=[hbm if k in far else vmem for k in range(len(args))],
        out_specs=jax.tree.map(lambda _: vmem, outs),
        scratch_shapes=scratch,
        cost_estimate=pl.CostEstimate(flops=flops, bytes_accessed=moved, transcendentals=0),
        compiler_params=pltpu.CompilerParams(vmem_limit_bytes=int(limit * 1024 * 1024)),
    )(*args)


def shards(head_inputs, b_proj, c_proj, log_decay, skip_gain, w_out, norm_gain, owner_ids):
    x, b, c, decays = head_inputs[0], b_proj[0], c_proj[0], log_decay.transpose(2, 0, 1)
    steps, width = x.shape
    heads = decays.shape[0]
    state_dim = b.shape[1]
    width_out = w_out.shape[1]
    times = lax.axis_size("tm")
    pieces = lax.axis_size("head")
    owners = times * lax.axis_size("farm")
    block = steps // pieces
    capacity = max(2, 2 * block // owners)
    depth = state_dim // times
    spec = jax.ShapeDtypeStruct
    wide = pltpu.VMEM((steps, width), BF16)
    narrow = pltpu.VMEM((steps, state_dim), BF16)
    state = pltpu.VMEM((state_dim, width), F32)
    parcel = call(
        state_kernel,
        spec((times, depth, width + LANES), BF16),
        [
            wide,
            narrow,
            pltpu.VMEM(decays.shape, F32),
            wide,
            state,
            pltpu.SemaphoreType.DMA((2 + steps // LANES,)),
        ],
        2 * steps * width * state_dim,
        2 * steps * width,
        63.4,
        x,
        b,
        decays,
        far=(0, 1, 2),
    )
    parcel = lax.all_to_all(parcel, "tm", split_axis=0, concat_axis=0, tiled=True)
    local = call(
        local_kernel,
        spec((steps + 2 * ROWS, width + state_dim), BF16),
        [
            wide,
            narrow,
            narrow,
            pltpu.VMEM(decays.shape, F32),
            state,
            pltpu.SemaphoreType.DMA((4,)),
        ],
        6 * steps * width * state_dim,
        8 * steps * width,
        61.5,
        x,
        b,
        c,
        decays,
        skip_gain[None, :],
        far=(0, 1, 2, 3),
    )
    parcel, local, w_late = lax.optimization_barrier((parcel, local, w_out))
    weights, local, target, gain = call(
        functools.partial(early_kernel, owners, capacity),
        (
            spec(w_out.shape, BF16),
            spec(local.shape, BF16),
            spec((1, block), jnp.int32),
            spec((1, width_out), F32),
        ),
        [pltpu.SemaphoreType.DMA((2,))],
        2 * owners * block * block,
        4 * width * width_out,
        16,
        w_late,
        local,
        owner_ids[0, :, 0][None, :],
        norm_gain[None, :],
        far=(0, 1),
    )
    prior = call(
        functools.partial(prefix_kernel, heads),
        spec((times, depth, width), BF16),
        [pltpu.VMEM((times, width), F32)],
        2 * state_dim * width * LANES,
        4 * state_dim * width,
        16,
        parcel,
    )
    prior = lax.all_to_all(prior, "tm", split_axis=0, concat_axis=0, tiled=True)
    parts = call(
        functools.partial(project_kernel, heads),
        spec((pieces, block, width_out), BF16),
        [wide],
        2 * steps * width * (width_out + state_dim),
        2 * steps * (width + width_out) + 2 * width * width_out,
        24,
        local,
        prior,
        weights,
    )
    parts = lax.all_to_all(parts, "head", split_axis=0, concat_axis=0, tiled=True)
    outgoing = call(
        regroup_kernel,
        spec((owners, capacity, width_out), BF16),
        [],
        2 * owners * capacity * block * width_out,
        12 * block * width_out,
        16,
        target,
        gain,
        parts,
    )
    result = lax.all_to_all(outgoing, ("tm", "farm"), split_axis=0, concat_axis=0, tiled=True)
    return result[None, None]


def solution(mesh):
    placed = (
        P("farm", "tm", "head"),
        P("farm", "tm", None),
        P("farm", "tm", None),
        P("farm", "tm", "head"),
        P("head"),
        P("head", None),
        P(),
        P("farm", ("tm", "head"), None),
    )
    return jax.shard_map(
        shards,
        mesh=mesh,
        in_specs=placed,
        out_specs=P(("tm", "farm"), "head", None, None, None),
        check_vma=False,
    )
```
